128 devices in a mesh: dp: 32 (over z, x, core), fs: 4 (over y).
Axes of the slice: x: 4, y: 4, z: 4, core: 2. Of those that a mesh axis runs over, the one named last changes fastest.
Arguments:
- tokens: bfloat16 [12288, 3584], P('dp', 'fs'), may hold values from -12 to 12
- cotangent: bfloat16 [12288, 3584], P('dp', 'fs'), may hold values from -6 to 6
- w_query: bfloat16 [3584, 3584], P('dp', 'fs'), may hold values from -0.09375 to 0.09375
- w_key: bfloat16 [3584, 512], P('dp', 'fs'), may hold values from -0.09375 to 0.09375
- w_value: bfloat16 [3584, 512], P('dp', 'fs'), may hold values from -0.09375 to 0.09375
- w_out: bfloat16 [3584, 3584], P('fs', 'dp'), may hold values from -0.09375 to 0.09375
- route: int32 [12288], replicated, may hold values from 0 to 12287, as said below
- doc_lengths: int32 [32, 2], P('dp'), may hold values from 1 to 288, 384 in all within a row
Outputs:
- out_home: bfloat16 [12288, 3584], P('dp', 'fs')
- grad_in: bfloat16 [12288, 3584], P('dp', 'fs')
- grad_wq: bfloat16 [3584, 3584], P('dp', 'fs')
- grad_wk: bfloat16 [3584, 512], P('dp', 'fs')
- grad_wv: bfloat16 [3584, 512], P('dp', 'fs')
- grad_wo: bfloat16 [3584, 3584], P('fs', 'dp')
The draws below stay inside these ranges and needn't reach their ends.
Inputs may be any that keep to these rules, and one draw needn't show every extreme that they name: route is a permutation; home block i sends exactly 384 // 32 rows to each planned block. `doc_lengths`: each row holds two responses whose lengths sum to 384.
All inputs are finite; a program needn't handle non-finite values.
Results may differ from the reference program's by a relative error of at most 0.025.
Values may be sent and summed in bfloat16 or wider, within the bound.
No kernel may reach another device: no remote copies, remote signals or barrier semaphores. Data moves between devices by JAX's collectives and lax.ppermute only.
A program may use at most 128 MiB of HBM per device.

```python
import math
import jax
import jax.numpy as jnp
import numpy as np
from jax import lax

D = 3584
HEADS = 28
KVH = 4
HS = 128
TOK_DEV = 384
NDOC = 2
TOKENS = 12288
N_DP = 32
N_FS = 4


def draw_tokens(key, part):
    key = jax.random.fold_in(key, 11)
    base = jnp.clip(jax.random.normal(key, (TOKENS, D), jnp.float32), -6.0, 6.0)
    return base.astype(jnp.bfloat16)


def draw_route(key, part):
    key = jax.random.fold_in(key, 23)
    count_dp = TOKENS // TOK_DEV
    piece_rows = TOK_DEV // count_dp
    key_one, key_two, key_three = jax.random.split(key, 3)
    orders = jax.vmap(lambda sub: jax.random.permutation(sub, TOK_DEV))(jax.random.split(key_one, count_dp))
    shifts = jax.random.randint(key_two, (count_dp,), 0, count_dp)
    section = orders // piece_rows
    within = orders % piece_rows
    target = (section + shifts[:, None]) % count_dp
    places = jax.vmap(lambda sub: jax.random.permutation(sub, TOK_DEV))(jax.random.split(key_three, count_dp))
    anchor = jnp.arange(count_dp, dtype=jnp.int32)[:, None]
    incoming = anchor * piece_rows + within
    landing = places[target, incoming]
    return (target * TOK_DEV + landing).reshape(-1).astype(jnp.int32)


def strengthened(values, key, source, target, parts, factor):
    owner, partner = [(jnp.arange(values.shape[axis_at]) // (values.shape[axis_at] // parts)).reshape([-1 if axis == axis_at else 1 for axis in range(values.ndim)]) for axis_at in (source, target)]
    chosen = jax.random.permutation(key, parts)[partner]
    strong = (owner == chosen) | (owner == (partner + parts // 2) % parts)
    return jnp.where(strong, factor * values, values)


def block_scale(stream_key, extent, pieces, smallest, high):
    loudness = 1.0
    for dim, blocks in pieces:
        draws = jax.random.uniform(jax.random.fold_in(jax.random.fold_in(stream_key, 6), dim), (blocks,), jnp.float32, smallest / len(pieces), high / len(pieces))
        loudness = loudness * jnp.repeat(jnp.exp(draws), extent[dim] // blocks).reshape((-1,) + (1,) * (len(extent) - 1 - dim))
    return loudness


def split_up(count, total, bound, slope):
    portions = [(1 << 20) // math.isqrt(rank ** slope) + 1 for rank in range(2, count + 1)]
    surplus, counts = total - bound - (count - 1), [1] * (count - 1)
    while surplus > 0:
        free = [i for i in range(count - 1) if counts[i] < bound]
        pool, left = sum([portions[i] for i in free]), surplus
        for i in free:
            addition = min(bound - counts[i], max(1, left * portions[i] // pool), surplus)
            counts[i] = counts[i] + addition
            surplus = surplus - addition
    return np.array([bound] + counts)


def ragged_sizes(rng, amount, total, reach, slope):
    if amount == 2:
        one = jax.random.randint(rng, (), max(1, total - reach), min(reach, total - 1) + 1)
        return jnp.stack([one, total - one])
    sizes = jnp.asarray(split_up(amount, total, reach, slope), jnp.int32)
    couples = (amount - 1) // 2
    source_of, taker = sizes[1:1 + 2 * couples:2], sizes[2:2 + 2 * couples:2]
    slack = jnp.minimum(source_of - 1, reach - taker)
    passed = jax.random.randint(jax.random.fold_in(rng, 1), (couples,), 0, 1 << 20) % (slack + 1)
    sizes = sizes.at[1:1 + 2 * couples:2].set(source_of - passed).at[2:2 + 2 * couples:2].set(taker + passed)
    return sizes[jax.random.permutation(jax.random.fold_in(rng, 2), amount)]


def noise(key, dims, scale, limit, cuts=(), kind=jnp.bfloat16):
    drawn = scale * jax.random.normal(key, dims, jnp.float32)
    if cuts:
        drawn = drawn * block_scale(key, dims, cuts, -0.22, 0.18)
    return jnp.clip(drawn, -limit, limit).astype(kind)


def noise_with(rng, shape, scale, bound, cuts, heavy, held_as=jnp.bfloat16):
    values = scale * jax.random.normal(rng, shape, jnp.float32)
    if cuts:
        values = values * block_scale(rng, shape, cuts, -0.22, 0.18)
    return jnp.clip(strengthened(values, jax.random.fold_in(rng, 3), *heavy), -bound, bound).astype(held_as)


def setup_inputs(seed: int = 0) -> dict:
    splits = jax.random.split(jax.random.key(seed), 9)
    tokens = draw_tokens(jax.random.fold_in(splits[8], 71), 0)
    cotangent = noise_with(splits[1], (TOKENS, D), 1.0, 6.0, ((0, 32), (1, 4)), (0, 1, 32, 2.75))
    w_query = noise(splits[2], (D, HEADS * HS), D ** -0.5, 0.09375, ((0, 32), (1, 4)))
    w_key = noise(splits[3], (D, KVH * HS), D ** -0.5, 0.09375, ((0, 32), (1, 4)))
    w_value = noise(splits[4], (D, KVH * HS), D ** -0.5, 0.09375, ((0, 32), (1, 4)))
    w_out = noise(splits[5], (HEADS * HS, D), (HEADS * HS) ** -0.5, 0.09375, ((0, 4), (1, 32)))
    route = draw_route(jax.random.fold_in(splits[8], 71), 0)
    doc_lengths = jax.vmap(lambda own: ragged_sizes(own, NDOC, TOK_DEV, 3 * TOK_DEV // 4, 2))(jax.random.split(splits[7], N_DP)).reshape((N_DP, NDOC)).astype(jnp.int32)
    return dict(tokens=tokens, cotangent=cotangent, w_query=w_query, w_key=w_key, w_value=w_value, w_out=w_out, route=route, doc_lengths=doc_lengths)


theta_base = 1000000.0


def doc_layout(lengths, count_rows):
    ends = jnp.cumsum(lengths).astype(jnp.int32)
    starts = ends - lengths
    rows = jnp.arange(count_rows, dtype=jnp.int32)
    doc_of = jnp.sum((rows[:, None] >= ends[None, :]).astype(jnp.int32), axis=1)
    which = doc_of[:, None] == jnp.arange(lengths.shape[0], dtype=jnp.int32)[None, :]
    start_of = jnp.sum(jnp.where(which, starts[None, :], 0), axis=1).astype(jnp.int32)
    position = rows - start_of
    allowed = (doc_of[:, None] == doc_of[None, :]) & (rows[None, :] <= rows[:, None])
    return position, allowed


def angles(position, width):
    freq = theta_base ** (-(jnp.arange(width // 2, dtype=jnp.float32) * 2.0) / width)
    phase = position.astype(jnp.float32)[:, None] * freq[None, :]
    return jnp.cos(phase), jnp.sin(phase)


def rotate(values, cosine, sine):
    half = values.shape[-1] // 2
    first = values[..., :half]
    second = values[..., half:]
    cos_b = cosine[:, None, :]
    sin_b = sine[:, None, :]
    return jnp.concatenate([first * cos_b - second * sin_b, second * cos_b + first * sin_b], axis=-1)


def unrotate(grads, cosine, sine):
    half = grads.shape[-1] // 2
    first = grads[..., :half]
    second = grads[..., half:]
    cos_b = cosine[:, None, :]
    sin_b = sine[:, None, :]
    return jnp.concatenate([first * cos_b + second * sin_b, second * cos_b - first * sin_b], axis=-1)


def attend_forward(query, keys, values, allowed, scale):
    scores = jnp.einsum("qcgd,kcd->cgqk", query.astype(jnp.float32), keys.astype(jnp.float32)) * scale
    scores = jnp.where(allowed[None, None], scores, -1e30)
    top = jnp.max(scores, axis=-1, keepdims=True)
    expo = jnp.exp(scores - top)
    probs = expo / jnp.sum(expo, axis=-1, keepdims=True)
    probs_low = probs.astype(jnp.bfloat16)
    attended = jnp.einsum("cgqk,kcd->qcgd", probs_low.astype(jnp.float32), values.astype(jnp.float32))
    return attended.astype(jnp.bfloat16), probs, probs_low


def attend_backward(query, keys, values, attended, d_att, probs, probs_low, scale):
    d_att_f = d_att.astype(jnp.float32)
    d_probs = jnp.einsum("qcgd,kcd->cgqk", d_att_f, values.astype(jnp.float32))
    delta = jnp.einsum("qcgd,qcgd->cgq", d_att_f, attended.astype(jnp.float32))
    d_scores = (probs * (d_probs - delta[..., None]) * scale).astype(jnp.bfloat16)
    d_scores_f = d_scores.astype(jnp.float32)
    d_query = jnp.einsum("cgqk,kcd->qcgd", d_scores_f, keys.astype(jnp.float32))
    d_keys = jnp.einsum("cgqk,qcgd->kcd", d_scores_f, query.astype(jnp.float32))
    d_values = jnp.einsum("cgqk,qcgd->kcd", probs_low.astype(jnp.float32), d_att_f)
    return d_query, d_keys, d_values.astype(jnp.bfloat16)


def rounded(term):
    return lax.optimization_barrier(term.astype(jnp.bfloat16)).astype(jnp.float32)


def reference(tokens, cotangent, w_query, w_key, w_value, w_out, route, doc_lengths):
    groups = HEADS // KVH
    scale = HS ** -0.5
    q_width = HEADS * HS // N_FS
    kv_width = KVH * HS // N_FS
    inverse = jnp.zeros((TOKENS,), jnp.int32).at[route].set(jnp.arange(TOKENS, dtype=jnp.int32))
    planned_x = tokens[inverse].reshape(N_DP, TOK_DEV, D)
    planned_c = cotangent[inverse].reshape(N_DP, TOK_DEV, D)

    def block(carry, inputs):
        x_rows, c_rows, lengths = inputs
        position, allowed = doc_layout(lengths, TOK_DEV)
        cosine, sine = angles(position, HS)
        q_pre = jnp.dot(x_rows, w_query, preferred_element_type=jnp.float32).reshape(TOK_DEV, HEADS, HS)
        query = rotate(q_pre, cosine, sine).astype(jnp.bfloat16).reshape(TOK_DEV, KVH, groups, HS)
        k_pre = jnp.dot(x_rows, w_key, preferred_element_type=jnp.float32).reshape(TOK_DEV, KVH, HS)
        keys = rotate(k_pre, cosine, sine).astype(jnp.bfloat16)
        values = jnp.dot(x_rows, w_value, preferred_element_type=jnp.float32).astype(jnp.bfloat16).reshape(TOK_DEV, KVH, HS)
        attended, probs, probs_low = attend_forward(query, keys, values, allowed, scale)
        flat = attended.reshape(TOK_DEV, HEADS * HS)
        out_sum = jnp.zeros((TOK_DEV, D), jnp.float32)
        for group in range(N_FS):
            lo_q = group * q_width
            out_sum = out_sum + rounded(jnp.dot(flat[:, lo_q:lo_q + q_width], w_out[lo_q:lo_q + q_width, :], preferred_element_type=jnp.float32))
        out_rows = out_sum.astype(jnp.bfloat16)
        d_att = jnp.dot(c_rows, w_out.T, preferred_element_type=jnp.float32).astype(jnp.bfloat16)
        d_att = d_att.reshape(TOK_DEV, KVH, groups, HS)
        d_query, d_keys, d_values = attend_backward(query, keys, values, attended, d_att, probs, probs_low, scale)
        dq_flat = unrotate(d_query.reshape(TOK_DEV, HEADS, HS), cosine, sine).astype(jnp.bfloat16).reshape(TOK_DEV, HEADS * HS)
        dk_flat = unrotate(d_keys, cosine, sine).astype(jnp.bfloat16).reshape(TOK_DEV, KVH * HS)
        dv_flat = d_values.reshape(TOK_DEV, KVH * HS)
        grad_sum = jnp.zeros((TOK_DEV, D), jnp.float32)
        for group in range(N_FS):
            lo_q = group * q_width
            lo_k = group * kv_width
            part = jnp.dot(dq_flat[:, lo_q:lo_q + q_width], w_query[:, lo_q:lo_q + q_width].T, preferred_element_type=jnp.float32)
            part = part + jnp.dot(dk_flat[:, lo_k:lo_k + kv_width], w_key[:, lo_k:lo_k + kv_width].T, preferred_element_type=jnp.float32)
            part = part + jnp.dot(dv_flat[:, lo_k:lo_k + kv_width], w_value[:, lo_k:lo_k + kv_width].T, preferred_element_type=jnp.float32)
            grad_sum = grad_sum + rounded(part)
        sum_q, sum_k, sum_v, sum_o = carry
        sum_q = sum_q + rounded(jnp.dot(x_rows.T, dq_flat, preferred_element_type=jnp.float32))
        sum_k = sum_k + rounded(jnp.dot(x_rows.T, dk_flat, preferred_element_type=jnp.float32))
        sum_v = sum_v + rounded(jnp.dot(x_rows.T, dv_flat, preferred_element_type=jnp.float32))
        sum_o = sum_o + rounded(jnp.dot(flat.T, c_rows, preferred_element_type=jnp.float32))
        return (sum_q, sum_k, sum_v, sum_o), (out_rows, grad_sum.astype(jnp.bfloat16))

    start = (jnp.zeros((D, HEADS * HS), jnp.float32), jnp.zeros((D, KVH * HS), jnp.float32),
             jnp.zeros((D, KVH * HS), jnp.float32), jnp.zeros((HEADS * HS, D), jnp.float32))
    sums, (out_planned, grad_planned) = lax.scan(block, start, (planned_x, planned_c, doc_lengths))
    out_home = out_planned.reshape(TOKENS, D)[route]
    return (out_home, grad_planned.reshape(TOKENS, D), sums[0].astype(jnp.bfloat16),
            sums[1].astype(jnp.bfloat16), sums[2].astype(jnp.bfloat16), sums[3].astype(jnp.bfloat16))
```

```python
import jax
import jax.numpy as jnp
from jax import lax
from jax.sharding import PartitionSpec as P

HS = 128
NZ, NX, NC = 4, 4, 2
theta_base = 1000000.0
f32 = jnp.float32
bf16 = jnp.bfloat16


def doc_layout(lengths, count_rows):
    ends = jnp.cumsum(lengths)
    starts = ends - lengths
    rows = jnp.arange(count_rows, dtype=jnp.int32)
    doc_of = jnp.sum((rows[:, None] >= ends[None, :]).astype(jnp.int32), axis=1)
    which = doc_of[:, None] == jnp.arange(lengths.shape[0], dtype=jnp.int32)[None, :]
    start_of = jnp.sum(jnp.where(which, starts[None, :], 0), axis=1)
    position = rows - start_of
    allowed = (doc_of[:, None] == doc_of[None, :]) & (rows[None, :] <= rows[:, None])
    return (position, allowed)


def angles(position, width):
    freq = theta_base ** (-(jnp.arange(width // 2, dtype=jnp.float32) * 2.0) / width)
    phase = position.astype(jnp.float32)[:, None] * freq[None, :]
    return (jnp.cos(phase), jnp.sin(phase))


def rotate(values, cosine, sine):
    half = values.shape[-1] // 2
    first = values[..., :half]
    second = values[..., half:]
    cos_b = cosine[:, None, :]
    sin_b = sine[:, None, :]
    return jnp.concatenate(
        [first * cos_b - second * sin_b, second * cos_b + first * sin_b], axis=-1
    )


def unrotate(grads, cosine, sine):
    return rotate(grads, cosine, -sine)


def attend_forward(query, keys, values, allowed, scale):
    scores = jnp.einsum("qcgd,kcd->cgqk", query, keys, preferred_element_type=f32) * scale
    scores = jnp.where(allowed[None, None], scores, -1e30)
    top = jnp.max(scores, axis=-1, keepdims=True)
    expo = jnp.exp(scores - top)
    probs = expo / jnp.sum(expo, axis=-1, keepdims=True)
    probs_low = probs.astype(bf16)
    attended = jnp.einsum("cgqk,kcd->qcgd", probs_low, values, preferred_element_type=f32)
    return (attended.astype(bf16), probs, probs_low)


def attend_backward(query, keys, values, attended, d_att, probs, probs_low, scale):
    d_probs = jnp.einsum("qcgd,kcd->cgqk", d_att, values, preferred_element_type=f32)
    delta = jnp.einsum("qcgd,qcgd->cgq", d_att, attended, preferred_element_type=f32)
    d_scores = (probs * (d_probs - delta[..., None]) * scale).astype(bf16)
    d_query = jnp.einsum("cgqk,kcd->qcgd", d_scores, keys, preferred_element_type=f32)
    d_keys = jnp.einsum("cgqk,qcgd->kcd", d_scores, query, preferred_element_type=f32)
    d_values = jnp.einsum("cgqk,qcgd->kcd", probs_low, d_att, preferred_element_type=f32)
    return (d_query, d_keys, d_values.astype(bf16))


def contract_rows(left, right):
    return lax.dot_general(left, right, (((0,), (0,)), ((), ())), preferred_element_type=f32)


def contract_cols(left, right):
    return lax.dot_general(left, right, (((1,), (1,)), ((), ())), preferred_element_type=f32)


def dp_index(z, x, c):
    return ((z % NZ) * NX + x % NX) * NC + c % NC


DP_ALL = [(z, x, c) for z in range(NZ) for x in range(NX) for c in range(NC)]
PERMS = {
    "z": lambda s: [(dp_index(z, x, c), dp_index(z + s, x, c)) for z, x, c in DP_ALL],
    "x": lambda s: [(dp_index(z, x, c), dp_index(z, x + s, c)) for z, x, c in DP_ALL],
    "core": lambda s: [(dp_index(z, x, c), dp_index(z, x, c + s)) for z, x, c in DP_ALL],
}


def shift(values, axis, step):
    if axis == "fs":
        return lax.ppermute(values, "fs", [(i, (i + step) % 4) for i in range(4)])
    return lax.ppermute(values, "dp", PERMS[axis](step))


def add(*terms):
    return sum([term.astype(f32) for term in terms]).astype(bf16)


def ring_gather(own, axis, split):
    below = shift(own, axis, 1)
    above = shift(own, axis, -1)
    far_one = shift(below[:split], axis, 1)
    far_two = shift(above[split:], axis, -1)
    return [own, above, jnp.concatenate([far_one, far_two], axis=0), below]


def ring_scatter(pieces, axis, split):
    down = shift(pieces[2][:split], axis, 1)
    up = shift(pieces[2][split:], axis, -1)
    one = jnp.concatenate([add(pieces[1][:split], down), pieces[1][split:]], axis=0)
    three = jnp.concatenate([pieces[3][:split], add(pieces[3][split:], up)], axis=0)
    return add(pieces[0], shift(one, axis, 1), shift(three, axis, -1))


def rolled(stack, start):
    return lax.dynamic_slice_in_dim(jnp.concatenate([stack, stack], axis=0), start % 4, 4, axis=0)


def local(tokens, cotangent, w_query, w_key, w_value, w_out, route, doc_lengths):
    count_dp = lax.axis_size("dp")
    my_index = lax.axis_index("dp")
    my_fs = lax.axis_index("fs")
    my_z, my_x, my_c = my_index // 8, (my_index // 2) % 4, my_index % 2
    count_rows, width = tokens.shape
    piece_rows = count_rows // count_dp
    shard = w_query.shape[0]
    scale = HS ** (-0.5)

    w_qkv = lax.all_gather(
        jnp.concatenate([w_query, w_key, w_value], axis=1), "dp", axis=0, tiled=True
    )
    w_out_t = lax.all_gather(w_out.T, "dp", axis=0, tiled=True)

    line_ids = jnp.arange(count_rows, dtype=jnp.int32)
    own_route = lax.dynamic_slice_in_dim(route, my_index * count_rows, count_rows)
    send_rank = jnp.sum((own_route[None, :] < own_route[:, None]).astype(jnp.int32), axis=1)
    send_table = (send_rank[None, :] == line_ids[:, None]).astype(bf16)

    planned = my_index * count_rows + line_ids
    home_block = jnp.arange(route.shape[0], dtype=jnp.int32) // count_rows
    source = jnp.sum(jnp.where(route[None, :] == planned[:, None], home_block[None, :], 0), axis=1)
    earlier = (source[None, :] == source[:, None]) & (line_ids[None, :] < line_ids[:, None])
    buffer_row = source * piece_rows + jnp.sum(earlier.astype(jnp.int32), axis=1)
    recv_table = (buffer_row[:, None] == line_ids[None, :]).astype(bf16)

    def outbound(values):
        moved = jnp.dot(send_table, values, preferred_element_type=f32).astype(bf16)
        return moved.reshape(count_dp, piece_rows, values.shape[1])

    def inbound(values):
        flat_in = values.reshape(count_rows, values.shape[2])
        return jnp.dot(recv_table, flat_in, preferred_element_type=f32).astype(bf16)

    def swap(values):
        return lax.all_to_all(values, "dp", split_axis=0, concat_axis=0, tiled=True)

    def whole(own):
        pieces = jnp.stack(ring_gather(own, "fs", count_rows // 2), axis=0)
        return rolled(pieces, 4 - my_fs)

    def flat_of(blocks):
        return blocks.transpose(1, 0, 2).reshape(count_rows, 4 * width)

    x_blocks = whole(inbound(swap(outbound(tokens))))
    x_full = flat_of(x_blocks)
    c_blocks = whole(inbound(swap(outbound(cotangent))))
    c_full = flat_of(c_blocks)

    heads_here = w_query.shape[1] // HS
    kv_here = w_key.shape[1] // HS
    groups = heads_here // kv_here
    q_width, kv_width = heads_here * HS, kv_here * HS
    position, allowed = doc_layout(doc_lengths[0], count_rows)
    cosine, sine = angles(position, HS)
    qkv = jnp.dot(x_full, w_qkv, preferred_element_type=f32)
    query = (
        rotate(qkv[:, :q_width].reshape(count_rows, heads_here, HS), cosine, sine)
        .astype(bf16)
        .reshape(count_rows, kv_here, groups, HS)
    )
    keys = rotate(
        qkv[:, q_width : q_width + kv_width].reshape(count_rows, kv_here, HS), cosine, sine
    ).astype(bf16)
    values = qkv[:, q_width + kv_width :].astype(bf16).reshape(count_rows, kv_here, HS)
    attended, probs, probs_low = attend_forward(query, keys, values, allowed, scale)
    flat = attended.reshape(count_rows, heads_here * HS)

    head_part = contract_cols(flat, w_out_t).astype(bf16)
    head_blocks = rolled(head_part.reshape(count_rows, 4, width).transpose(1, 0, 2), my_fs)
    out_planned = ring_scatter(
        [head_blocks[r] for r in range(4)], "fs", count_rows // 2
    )
    going_home = contract_rows(recv_table, out_planned).astype(bf16)
    returned = swap(going_home.reshape(count_dp, piece_rows, width)).reshape(count_rows, width)
    out_home = contract_rows(send_table, returned).astype(bf16)

    d_att = (
        jnp.dot(c_full, w_out_t, preferred_element_type=f32)
        .astype(bf16)
        .reshape(count_rows, kv_here, groups, HS)
    )
    grad_out_part = contract_rows(c_full, flat).astype(bf16)
    wo_sum = lax.psum_scatter(grad_out_part, "dp", scatter_dimension=0, tiled=True).T

    d_query, d_keys, d_values = attend_backward(
        query, keys, values, attended, d_att, probs, probs_low, scale
    )
    dq_flat = unrotate(d_query.reshape(count_rows, heads_here, HS), cosine, sine).astype(bf16)
    dk_flat = unrotate(d_keys, cosine, sine).astype(bf16)
    d_qkv = jnp.concatenate(
        [
            dq_flat.reshape(count_rows, q_width),
            dk_flat.reshape(count_rows, kv_width),
            d_values.reshape(count_rows, kv_width),
        ],
        axis=1,
    )

    order = jnp.arange(width, dtype=jnp.int32)
    rel_c, rel_x, lane = order // (4 * shard), (order // shard) % 4, order % shard
    feature = ((my_x + rel_x) % 4 * 2 + (my_c + rel_c) % 2) * shard + lane
    pick = (feature[:, None] == order[None, :]).astype(bf16)
    x_by_z = rolled(x_blocks, my_z)
    x_rel = [contract_cols(pick, x_by_z[r]).astype(bf16) for r in range(4)]
    half = 4 * shard
    x_own = jnp.concatenate([block[:half] for block in x_rel], axis=0)
    x_other = jnp.concatenate([block[half:] for block in x_rel], axis=0)

    def x_major(rows):
        return rows.reshape(4, 4, shard, count_rows).transpose(1, 0, 2, 3).reshape(-1, count_rows)

    cut = 5 * HS

    def reduced(own_rows, other_rows, cols, first, second):
        there = jnp.dot(other_rows, cols, preferred_element_type=f32).astype(bf16)
        came = shift(there, "core", 1)
        here = jnp.dot(own_rows, cols, preferred_element_type=f32).astype(bf16)
        both = add(here, came).reshape(4, 4, shard, cols.shape[1])
        line = ring_scatter([both[r] for r in range(4)], first, 2)
        return ring_scatter([line[r] for r in range(4)], second, 64)

    part_a = reduced(x_own, x_other, d_qkv[:, :cut], "z", "x")
    part_b = reduced(x_major(x_own), x_major(x_other), d_qkv[:, cut:], "x", "z")
    grad_q = jnp.concatenate([part_a, part_b[:, : q_width - cut]], axis=1)
    grad_k = part_b[:, q_width - cut : q_width - cut + kv_width]
    grad_v = part_b[:, q_width - cut + kv_width :]

    grad_rows = contract_cols(d_qkv, w_qkv).astype(bf16)
    grad_blocks = rolled(grad_rows.reshape(count_rows, 4, width).transpose(1, 0, 2), my_fs)
    grad_in = ring_scatter([grad_blocks[r] for r in range(4)], "fs", count_rows // 2)

    return (out_home, grad_in, grad_q, grad_k, grad_v, wo_sum)


def solution(mesh):
    in_specs = (
        P("dp", "fs"),
        P("dp", "fs"),
        P("dp", "fs"),
        P("dp", "fs"),
        P("dp", "fs"),
        P("fs", "dp"),
        P(),
        P("dp", None),
    )
    out_specs = (
        P("dp", "fs"),
        P("dp", "fs"),
        P("dp", "fs"),
        P("dp", "fs"),
        P("dp", "fs"),
        P("fs", "dp"),
    )
    return jax.shard_map(local, mesh=mesh, in_specs=in_specs, out_specs=out_specs, check_vma=False)
```

```python
import jax
import jax.numpy as jnp
from jax import lax
from jax.sharding import PartitionSpec as P

HS = 128
NZ, NX, NC = 4, 4, 2
theta_base = 1000000.0
f32 = jnp.float32
bf16 = jnp.bfloat16


def doc_layout(lengths, count_rows):
    ends = jnp.cumsum(lengths)
    starts = ends - lengths
    rows = jnp.arange(count_rows, dtype=jnp.int32)
    doc_of = jnp.sum((rows[:, None] >= ends[None, :]).astype(jnp.int32), axis=1)
    which = doc_of[:, None] == jnp.arange(lengths.shape[0], dtype=jnp.int32)[None, :]
    start_of = jnp.sum(jnp.where(which, starts[None, :], 0), axis=1)
    position = rows - start_of
    allowed = (doc_of[:, None] == doc_of[None, :]) & (rows[None, :] <= rows[:, None])
    return (position, allowed)


def angles(position, width):
    freq = theta_base ** (-(jnp.arange(width // 2, dtype=jnp.float32) * 2.0) / width)
    phase = position.astype(jnp.float32)[:, None] * freq[None, :]
    return (jnp.cos(phase), jnp.sin(phase))


def rotate(values, cosine, sine):
    half = values.shape[-1] // 2
    first = values[..., :half]
    second = values[..., half:]
    cos_b = cosine[:, None, :]
    sin_b = sine[:, None, :]
    return jnp.concatenate(
        [first * cos_b - second * sin_b, second * cos_b + first * sin_b], axis=-1
    )


def unrotate(grads, cosine, sine):
    return rotate(grads, cosine, -sine)


def attend_forward(query, keys, values, allowed, scale):
    scores = jnp.einsum("qcgd,kcd->cgqk", query, keys, preferred_element_type=f32) * scale
    scores = jnp.where(allowed[None, None], scores, -1e30)
    top = jnp.max(scores, axis=-1, keepdims=True)
    expo = jnp.exp(scores - top)
    probs = expo / jnp.sum(expo, axis=-1, keepdims=True)
    probs_low = probs.astype(bf16)
    attended = jnp.einsum("cgqk,kcd->qcgd", probs_low, values, preferred_element_type=f32)
    return (attended.astype(bf16), probs, probs_low)


def attend_backward(query, keys, values, attended, d_att, probs, probs_low, scale):
    d_probs = jnp.einsum("qcgd,kcd->cgqk", d_att, values, preferred_element_type=f32)
    delta = jnp.einsum("qcgd,qcgd->cgq", d_att, attended, preferred_element_type=f32)
    d_scores = (probs * (d_probs - delta[..., None]) * scale).astype(bf16)
    d_query = jnp.einsum("cgqk,kcd->qcgd", d_scores, keys, preferred_element_type=f32)
    d_keys = jnp.einsum("cgqk,qcgd->kcd", d_scores, query, preferred_element_type=f32)
    d_values = jnp.einsum("cgqk,qcgd->kcd", probs_low, d_att, preferred_element_type=f32)
    return (d_query, d_keys, d_values.astype(bf16))


def contract_rows(left, right):
    return lax.dot_general(left, right, (((0,), (0,)), ((), ())), preferred_element_type=f32)


def contract_cols(left, right):
    return lax.dot_general(left, right, (((1,), (1,)), ((), ())), preferred_element_type=f32)


def dp_index(z, x, c):
    return ((z % NZ) * NX + x % NX) * NC + c % NC


DP_ALL = [(z, x, c) for z in range(NZ) for x in range(NX) for c in range(NC)]
PERMS = {
    "z": lambda s: [(dp_index(z, x, c), dp_index(z + s, x, c)) for z, x, c in DP_ALL],
    "x": lambda s: [(dp_index(z, x, c), dp_index(z, x + s, c)) for z, x, c in DP_ALL],
    "core": lambda s: [(dp_index(z, x, c), dp_index(z, x, c + s)) for z, x, c in DP_ALL],
}


def shift(values, axis, step):
    if axis == "fs":
        return lax.ppermute(values, "fs", [(i, (i + step) % 4) for i in range(4)])
    return lax.ppermute(values, "dp", PERMS[axis](step))


def add(*terms):
    return sum([term.astype(f32) for term in terms]).astype(bf16)


def ring_first(own, axis):
    return shift(own, axis, 1), shift(own, axis, -1)


def ring_gather(own, first, axis, split):
    below, above = first
    far_one = shift(below[:split], axis, 1)
    far_two = shift(above[split:], axis, -1)
    return [own, above, jnp.concatenate([far_one, far_two], axis=0), below]


def ring_scatter(pieces, axis, split):
    down = shift(pieces[2][:split], axis, 1)
    up = shift(pieces[2][split:], axis, -1)
    one = jnp.concatenate([add(pieces[1][:split], down), pieces[1][split:]], axis=0)
    three = jnp.concatenate([pieces[3][:split], add(pieces[3][split:], up)], axis=0)
    return add(pieces[0], shift(one, axis, 1), shift(three, axis, -1))


def rolled(stack, start):
    return lax.dynamic_slice_in_dim(jnp.concatenate([stack, stack], axis=0), start % 4, 4, axis=0)


def local(tokens, cotangent, w_query, w_key, w_value, w_out, route, doc_lengths):
    count_dp = lax.axis_size("dp")
    my_index = lax.axis_index("dp")
    my_fs = lax.axis_index("fs")
    my_z, my_x, my_c = my_index // 8, (my_index // 2) % 4, my_index % 2
    count_rows, width = tokens.shape
    piece_rows = count_rows // count_dp
    shard = w_query.shape[0]
    scale = HS ** (-0.5)

    w_qkv = lax.all_gather(
        jnp.concatenate([w_query, w_key, w_value], axis=1), "dp", axis=0, tiled=True
    )
    w_out_t = lax.all_gather(w_out.T, "dp", axis=0, tiled=True)

    line_ids = jnp.arange(count_rows, dtype=jnp.int32)
    own_route = lax.dynamic_slice_in_dim(route, my_index * count_rows, count_rows)
    send_rank = jnp.sum((own_route[None, :] < own_route[:, None]).astype(jnp.int32), axis=1)
    send_table = (send_rank[None, :] == line_ids[:, None]).astype(bf16)

    planned = my_index * count_rows + line_ids
    home_block = jnp.arange(route.shape[0], dtype=jnp.int32) // count_rows
    source = jnp.sum(jnp.where(route[None, :] == planned[:, None], home_block[None, :], 0), axis=1)
    earlier = (source[None, :] == source[:, None]) & (line_ids[None, :] < line_ids[:, None])
    buffer_row = source * piece_rows + jnp.sum(earlier.astype(jnp.int32), axis=1)
    recv_table = (buffer_row[:, None] == line_ids[None, :]).astype(bf16)

    def outbound(values):
        moved = jnp.dot(send_table, values, preferred_element_type=f32).astype(bf16)
        return moved.reshape(count_dp, piece_rows, values.shape[1])

    def inbound(values):
        flat_in = values.reshape(count_rows, values.shape[2])
        return jnp.dot(recv_table, flat_in, preferred_element_type=f32).astype(bf16)

    def swap(values):
        return lax.all_to_all(values, "dp", split_axis=0, concat_axis=0, tiled=True)

    def summed(blocks, axis_name):
        came = lax.all_to_all(blocks, axis_name, split_axis=0, concat_axis=0, tiled=True)
        return add(*[came[r] for r in range(4)])

    def whole(own, first):
        pieces = jnp.stack(ring_gather(own, first, "fs", count_rows // 2), axis=0)
        return rolled(pieces, 4 - my_fs)

    def flat_of(blocks):
        return blocks.transpose(1, 0, 2).reshape(count_rows, 4 * width)

    x_own = inbound(swap(outbound(tokens)))
    x_first = ring_first(x_own, "fs")
    x_blocks = whole(x_own, x_first)
    x_full = flat_of(x_blocks)
    c_out, x_first = lax.optimization_barrier((outbound(cotangent), x_first))
    c_own = inbound(swap(c_out))
    c_blocks = whole(c_own, ring_first(c_own, "fs"))
    c_full = flat_of(c_blocks)

    heads_here = w_query.shape[1] // HS
    kv_here = w_key.shape[1] // HS
    groups = heads_here // kv_here
    q_width, kv_width = heads_here * HS, kv_here * HS
    position, allowed = doc_layout(doc_lengths[0], count_rows)
    cosine, sine = angles(position, HS)
    qkv = jnp.dot(x_full, w_qkv, preferred_element_type=f32)
    query = (
        rotate(qkv[:, :q_width].reshape(count_rows, heads_here, HS), cosine, sine)
        .astype(bf16)
        .reshape(count_rows, kv_here, groups, HS)
    )
    keys = rotate(
        qkv[:, q_width : q_width + kv_width].reshape(count_rows, kv_here, HS), cosine, sine
    ).astype(bf16)
    values = qkv[:, q_width + kv_width :].astype(bf16).reshape(count_rows, kv_here, HS)
    attended, probs, probs_low = attend_forward(query, keys, values, allowed, scale)
    flat = attended.reshape(count_rows, heads_here * HS)

    head_part = contract_cols(flat, w_out_t).astype(bf16)
    out_planned = summed(head_part.reshape(count_rows, 4, width).transpose(1, 0, 2), "fs")
    going_home = contract_rows(recv_table, out_planned).astype(bf16)
    returned = swap(going_home.reshape(count_dp, piece_rows, width)).reshape(count_rows, width)
    out_home = contract_rows(send_table, returned).astype(bf16)

    d_att = (
        jnp.dot(c_full, w_out_t, preferred_element_type=f32)
        .astype(bf16)
        .reshape(count_rows, kv_here, groups, HS)
    )
    grad_out_part = contract_rows(c_full, flat).astype(bf16)
    wo_sum = lax.psum_scatter(grad_out_part, "dp", scatter_dimension=0, tiled=True).T

    d_query, d_keys, d_values = attend_backward(
        query, keys, values, attended, d_att, probs, probs_low, scale
    )
    dq_flat = unrotate(d_query.reshape(count_rows, heads_here, HS), cosine, sine).astype(bf16)
    dk_flat = unrotate(d_keys, cosine, sine).astype(bf16)
    d_qkv = jnp.concatenate(
        [
            dq_flat.reshape(count_rows, q_width),
            dk_flat.reshape(count_rows, kv_width),
            d_values.reshape(count_rows, kv_width),
        ],
        axis=1,
    )

    order = jnp.arange(width, dtype=jnp.int32)
    rel_c, at_x, lane = order // (4 * shard), (order // shard) % 4, order % shard
    feature = (at_x * 2 + (my_c + rel_c) % 2) * shard + lane
    pick = (feature[:, None] == order[None, :]).astype(bf16)
    x_t = jnp.stack([contract_cols(pick, x_blocks[j]).astype(bf16) for j in range(4)], axis=0)
    x_t = x_t.reshape(4, 2, 4, shard, count_rows)
    own_t, other_t = x_t[:, 0], x_t[:, 1]

    def relative(rows):
        return rolled(rolled(rows, my_z).transpose(1, 0, 2, 3), my_x)

    cut = 5 * HS

    def paired(own_rows, other_rows, cols):
        there = jnp.dot(other_rows.reshape(-1, count_rows), cols, preferred_element_type=f32)
        came = shift(there.astype(bf16), "core", 1)
        here = jnp.dot(own_rows.reshape(-1, count_rows), cols, preferred_element_type=f32)
        return add(here.astype(bf16), came).reshape(4, 4, shard, cols.shape[1])

    def summed_dp(blocks, axis):
        other = (lambda i: i % 8) if axis == "z" else (lambda i: i // 8 * 2 + i % 2)
        lines = [[i for i in range(count_dp) if other(i) == k] for k in range(8)]
        came = lax.all_to_all(
            blocks, "dp", split_axis=0, concat_axis=0, tiled=True, axis_index_groups=lines
        )
        return add(*[came[r] for r in range(4)])

    part_a = summed_dp(summed_dp(paired(own_t, other_t, d_qkv[:, :cut]), "z"), "x")
    both = paired(relative(own_t), relative(other_t), d_qkv[:, cut:])
    line = ring_scatter([both[r] for r in range(4)], "x", 2)
    part_b = ring_scatter([line[r] for r in range(4)], "z", 64)
    grad_q = jnp.concatenate([part_a, part_b[:, : q_width - cut]], axis=1)
    grad_k = part_b[:, q_width - cut : q_width - cut + kv_width]
    grad_v = part_b[:, q_width - cut + kv_width :]

    grad_rows = contract_cols(d_qkv, w_qkv).astype(bf16)
    grad_blocks = rolled(grad_rows.reshape(count_rows, 4, width).transpose(1, 0, 2), my_fs)
    grad_in = ring_scatter([grad_blocks[r] for r in range(4)], "fs", count_rows // 2)

    return (out_home, grad_in, grad_q, grad_k, grad_v, wo_sum)


def solution(mesh):
    in_specs = (
        P("dp", "fs"),
        P("dp", "fs"),
        P("dp", "fs"),
        P("dp", "fs"),
        P("dp", "fs"),
        P("fs", "dp"),
        P(),
        P("dp", None),
    )
    out_specs = (
        P("dp", "fs"),
        P("dp", "fs"),
        P("dp", "fs"),
        P("dp", "fs"),
        P("dp", "fs"),
        P("fs", "dp"),
    )
    return jax.shard_map(local, mesh=mesh, in_specs=in_specs, out_specs=out_specs, check_vma=False)
```

```python
import jax
import jax.numpy as jnp
from jax import lax
from jax.experimental import pallas as pl
from jax.experimental.pallas import tpu as pltpu
from jax.sharding import PartitionSpec as P

HS = 128
NZ, NX, NC = 4, 4, 2
theta_base = 1000000.0
f32 = jnp.float32
bf16 = jnp.bfloat16


def angles(position, width):
    freq = theta_base ** (-(jnp.arange(width // 2, dtype=jnp.float32) * 2.0) / width)
    phase = position.astype(jnp.float32)[:, None] * freq[None, :]
    return (jnp.cos(phase), jnp.sin(phase))


def rotated(values, cosine, sine):
    return values * cosine + pltpu.roll(values, HS // 2, 1) * sine


def unrotated(values, cosine, sine):
    return values * cosine - pltpu.roll(values, HS // 2, 1) * sine


def mask_of(first_length, count_rows):
    row = lax.broadcasted_iota(jnp.int32, (count_rows, count_rows), 0)
    col = lax.broadcasted_iota(jnp.int32, (count_rows, count_rows), 1)
    return (col <= row) & ((row >= first_length) == (col >= first_length))


def probs_of(query, keys, allowed):
    scores = nt(query, keys) * (HS ** (-0.5))
    scores = jnp.where(allowed, scores, -1e30)
    expo = jnp.exp(scores - jnp.max(scores, axis=-1, keepdims=True))
    return expo / jnp.sum(expo, axis=-1, keepdims=True)


def nt(left, right):
    return lax.dot_general(left, right, (((1,), (1,)), ((), ())), preferred_element_type=f32)


def tn(left, right):
    return lax.dot_general(left, right, (((0,), (0,)), ((), ())), preferred_element_type=f32)


def nn(left, right):
    return jnp.dot(left, right, preferred_element_type=f32)


def accumulate(step, pieces, w_ref, acc):
    own, above, far_one, far_two, below = pieces
    half = far_one.shape[0]

    @pl.when(step == 0)
    def _():
        acc[...] = nn(own[...], w_ref[...])

    @pl.when(step == 1)
    def _():
        acc[...] += nn(above[...], w_ref[...])

    @pl.when(step == 2)
    def _():
        acc[:half] += nn(far_one[...], w_ref[...])
        acc[half:] += nn(far_two[...], w_ref[...])

    @pl.when(step == 3)
    def _():
        acc[...] += nn(below[...], w_ref[...])


def forward_kernel(info, own, above, far_one, far_two, below, w_ref, cos_ref, sin_ref,
                   q_ref, k_ref, v_ref, flat_ref, acc):
    step = pl.program_id(0)
    accumulate(step, (own, above, far_one, far_two, below), w_ref, acc)
    count_rows, q_width = q_ref.shape

    @pl.when(step == 3)
    def _():
        cosine, sine = cos_ref[...], sin_ref[...]
        keys = rotated(acc[:, q_width : q_width + HS], cosine, sine).astype(bf16)
        values = acc[:, q_width + HS :].astype(bf16)
        k_ref[...] = keys
        v_ref[...] = values
        allowed = mask_of(info[1], count_rows)
        for head in range(q_width // HS):
            cols = slice(head * HS, (head + 1) * HS)
            query = rotated(acc[:, cols], cosine, sine).astype(bf16)
            q_ref[:, cols] = query
            low = probs_of(query, keys, allowed).astype(bf16)
            flat_ref[:, cols] = nn(low, values).astype(bf16)


def backward_kernel(info, own, above, far_one, far_two, below, w_ref, cos_ref, sin_ref,
                    q_ref, k_ref, v_ref, flat_ref, grad_ref, acc):
    step = pl.program_id(0)
    accumulate(step, (own, above, far_one, far_two, below), w_ref, acc)
    count_rows, q_width = q_ref.shape

    @pl.when(step == 3)
    def _():
        cosine, sine = cos_ref[...], sin_ref[...]
        keys, values = k_ref[...], v_ref[...]
        allowed = mask_of(info[1], count_rows)
        d_keys = jnp.zeros((count_rows, HS), f32)
        d_values = jnp.zeros((count_rows, HS), f32)
        for head in range(q_width // HS):
            cols = slice(head * HS, (head + 1) * HS)
            query = q_ref[:, cols]
            d_att = acc[:, cols].astype(bf16)
            probs = probs_of(query, keys, allowed)
            delta = jnp.sum(
                d_att.astype(f32) * flat_ref[:, cols].astype(f32), axis=-1, keepdims=True
            )
            d_probs = nt(d_att, values)
            d_scores = (probs * (d_probs - delta) * (HS ** (-0.5))).astype(bf16)
            d_values += tn(probs.astype(bf16), d_att)
            d_keys += tn(d_scores, query)
            grad_ref[:, cols] = unrotated(nn(d_scores, keys), cosine, sine).astype(bf16)
        grad_ref[:, q_width : q_width + HS] = unrotated(d_keys, cosine, sine).astype(bf16)
        grad_ref[:, q_width + HS :] = d_values.astype(bf16)


def blocks_kernel(left_ref, w_ref, out_ref):
    out_ref[0] = nt(left_ref[...], w_ref[...]).astype(bf16)


def grad_out_kernel(info, own, above, far_one, far_two, below, flat_ref, out_ref):
    step = pl.program_id(0)
    half = far_one.shape[0]

    @pl.when(step == 0)
    def _():
        out_ref[...] = tn(own[...], flat_ref[...]).astype(bf16)

    @pl.when(step == 1)
    def _():
        out_ref[...] = tn(above[...], flat_ref[...]).astype(bf16)

    @pl.when(step == 2)
    def _():
        total = tn(far_one[...], flat_ref[:half]) + tn(far_two[...], flat_ref[half:])
        out_ref[...] = total.astype(bf16)

    @pl.when(step == 3)
    def _():
        out_ref[...] = tn(below[...], flat_ref[...]).astype(bf16)


def transpose_kernel(info, own, above, far_one, far_two, below, out_ref):
    step = pl.program_id(0)
    shard = out_ref.shape[3]

    def put(piece):
        turned = piece.T
        for at_x in range(4):
            for at_c in range(2):
                start = (at_x * 2 + at_c) * shard
                out_ref[(at_c + info[4]) % 2, 0, (at_x + 4 - info[3]) % 4] = (
                    turned[start : start + shard]
                )

    @pl.when(step == 0)
    def _():
        put(own[...])

    @pl.when(step == 1)
    def _():
        put(above[...])

    @pl.when(step == 2)
    def _():
        put(jnp.concatenate([far_one[...], far_two[...]], axis=0))

    @pl.when(step == 3)
    def _():
        put(below[...])


def fixed(array):
    zeros = (0,) * array.ndim
    return pl.BlockSpec(array.shape, lambda *_: zeros)


PARAMS = dict(compiler_params=pltpu.CompilerParams(vmem_limit_bytes=48 * 1024 * 1024))


def shape_of(*dims):
    return jax.ShapeDtypeStruct(dims, bf16)


def by_piece(kernel, info, operands, w, outs, out_specs, scratch):
    specs = [fixed(operand) for operand in operands]
    if w is not None:
        block = w.shape[0] // 4
        operands = operands[:5] + [w] + operands[5:]
        specs = specs[:5] + [
            pl.BlockSpec((block, w.shape[1]), lambda k, s: ((s[0] + k) % 4, 0))
        ] + specs[5:]
    return pl.pallas_call(
        kernel,
        out_shape=outs,
        grid_spec=pltpu.PrefetchScalarGridSpec(
            num_scalar_prefetch=1, grid=(4,), in_specs=specs, out_specs=out_specs,
            scratch_shapes=scratch,
        ),
        **PARAMS,
    )(info, *operands)


def by_block(left, w):
    block = w.shape[0] // 4
    return pl.pallas_call(
        blocks_kernel,
        out_shape=shape_of(4, left.shape[0], block),
        grid=(4,),
        in_specs=[fixed(left), pl.BlockSpec((block, w.shape[1]), lambda k: (k, 0))],
        out_specs=pl.BlockSpec((1, left.shape[0], block), lambda k: (k, 0, 0)),
        **PARAMS,
    )(left, w)


def dp_index(z, x, c):
    return ((z % NZ) * NX + x % NX) * NC + c % NC


DP_ALL = [(z, x, c) for z in range(NZ) for x in range(NX) for c in range(NC)]
PERMS = {
    "z": lambda s: [(dp_index(z, x, c), dp_index(z + s, x, c)) for z, x, c in DP_ALL],
    "x": lambda s: [(dp_index(z, x, c), dp_index(z, x + s, c)) for z, x, c in DP_ALL],
    "core": lambda s: [(dp_index(z, x, c), dp_index(z, x, c + s)) for z, x, c in DP_ALL],
}


def shift(values, axis, step):
    if axis == "fs":
        return lax.ppermute(values, "fs", [(i, (i + step) % 4) for i in range(4)])
    return lax.ppermute(values, "dp", PERMS[axis](step))


def add(*terms):
    return sum([term.astype(f32) for term in terms]).astype(bf16)


def ring_first(own, axis):
    return shift(own, axis, 1), shift(own, axis, -1)


def ring_rest(own, first, axis):
    below, above = first
    half = own.shape[0] // 2
    return [own, above, shift(below[:half], axis, 1), shift(above[half:], axis, -1), below]


def ring_scatter(pieces, axis, split):
    down = shift(pieces[2][:split], axis, 1)
    up = shift(pieces[2][split:], axis, -1)
    one = jnp.concatenate([add(pieces[1][:split], down), pieces[1][split:]], axis=0)
    three = jnp.concatenate([pieces[3][:split], add(pieces[3][split:], up)], axis=0)
    return add(pieces[0], shift(one, axis, 1), shift(three, axis, -1))


def after(values, first):
    return lax.optimization_barrier((values, first))[0]


def local(tokens, cotangent, w_query, w_key, w_value, w_out, route, doc_lengths):
    count_dp = lax.axis_size("dp")
    my_index = lax.axis_index("dp")
    my_fs = lax.axis_index("fs")
    my_z, my_x, my_c = my_index // 8, (my_index // 2) % 4, my_index % 2
    count_rows, width = tokens.shape
    piece_rows = count_rows // count_dp
    shard = w_query.shape[0]
    q_width, kv_width = w_query.shape[1], w_key.shape[1]

    w_qkv = lax.all_gather(
        jnp.concatenate([w_query, w_key, w_value], axis=1), "dp", axis=0, tiled=True
    )
    w_out_t = lax.all_gather(w_out.T, "dp", axis=0, tiled=True)

    line_ids = jnp.arange(count_rows, dtype=jnp.int32)
    own_route = lax.dynamic_slice_in_dim(route, my_index * count_rows, count_rows)
    send_rank = jnp.sum((own_route[None, :] < own_route[:, None]).astype(jnp.int32), axis=1)
    send_table = (send_rank[None, :] == line_ids[:, None]).astype(bf16)

    planned = my_index * count_rows + line_ids
    home_block = jnp.arange(route.shape[0], dtype=jnp.int32) // count_rows
    source = jnp.sum(jnp.where(route[None, :] == planned[:, None], home_block[None, :], 0), axis=1)
    earlier = (source[None, :] == source[:, None]) & (line_ids[None, :] < line_ids[:, None])
    buffer_row = source * piece_rows + jnp.sum(earlier.astype(jnp.int32), axis=1)
    recv_table = (buffer_row[:, None] == line_ids[None, :]).astype(bf16)

    def outbound(values):
        moved = nn(send_table, values).astype(bf16)
        return moved.reshape(count_dp, piece_rows, values.shape[1])

    def inbound(values):
        return nn(recv_table, values.reshape(count_rows, values.shape[2])).astype(bf16)

    def swap(values):
        return lax.all_to_all(values, "dp", split_axis=0, concat_axis=0, tiled=True)

    def summed(blocks, axis_name):
        came = lax.all_to_all(blocks, axis_name, split_axis=0, concat_axis=0, tiled=True)
        return add(*[came[r] for r in range(4)])

    first_length = doc_lengths[0, 0]
    position = line_ids - jnp.where(line_ids >= first_length, first_length, 0)
    cosine, sine = angles(position, HS)
    cosine = jnp.concatenate([cosine, cosine], axis=1)
    sine = jnp.concatenate([-sine, sine], axis=1)
    info = jnp.stack([my_fs, first_length, my_z, my_x, my_c]).astype(jnp.int32)

    x_own = inbound(swap(outbound(tokens)))
    x_first = ring_first(x_own, "fs")
    c_recv = swap(after(outbound(cotangent), x_first))
    x_pieces = ring_rest(x_own, x_first, "fs")

    rows_of = lambda cols: pl.BlockSpec((count_rows, cols), lambda *_: (0, 0))
    query, keys, values, flat = by_piece(
        forward_kernel, info, x_pieces + [cosine, sine], w_qkv,
        (shape_of(count_rows, q_width), shape_of(count_rows, kv_width),
         shape_of(count_rows, kv_width), shape_of(count_rows, q_width)),
        (rows_of(q_width), rows_of(kv_width), rows_of(kv_width), rows_of(q_width)),
        [pltpu.VMEM((count_rows, q_width + 2 * kv_width), f32)],
    )

    c_own = inbound(after(c_recv, flat))
    c_pieces = ring_rest(c_own, ring_first(c_own, "fs"), "fs")

    x_turned = by_piece(
        transpose_kernel, info, after(x_pieces, flat), None,
        shape_of(2, 4, 4, shard, count_rows),
        pl.BlockSpec((2, 1, 4, shard, count_rows), lambda k, s: (0, (s[0] + k + 4 - s[2]) % 4, 0, 0, 0)),
        [],
    )

    grad_out_part = by_piece(
        grad_out_kernel, info, c_pieces + [flat], None,
        shape_of(4 * width, q_width),
        pl.BlockSpec((width, q_width), lambda k, s: ((s[0] + k) % 4, 0)),
        [],
    )
    wo_sum = lax.psum_scatter(grad_out_part, "dp", scatter_dimension=0, tiled=True).T

    head_blocks = by_block(flat, w_out_t)
    out_planned = summed(head_blocks, "fs")

    d_qkv = by_piece(
        backward_kernel, info,
        after(c_pieces, head_blocks) + [cosine, sine, query, keys, values, flat], w_out_t,
        shape_of(count_rows, q_width + 2 * kv_width), rows_of(q_width + 2 * kv_width),
        [pltpu.VMEM((count_rows, q_width), f32)],
    )

    own_t, other_t = [x_turned[i].reshape(16 * shard, count_rows) for i in range(2)]
    cut = 5 * HS
    there = [nn(other_t, cols).astype(bf16) for cols in (d_qkv[:, :cut], d_qkv[:, cut:])]
    came = [shift(block, "core", 1) for block in there]
    own_t = after(own_t, there)
    both = [
        add(nn(own_t, cols).astype(bf16), block).reshape(4, 4, shard, cols.shape[1])
        for cols, block in zip((d_qkv[:, :cut], d_qkv[:, cut:]), came)
    ]
    line_a = ring_scatter([both[0][r] for r in range(4)], "z", 2)
    line_b = ring_scatter([both[1][:, r] for r in range(4)], "x", 2)
    part_a = ring_scatter([line_a[r] for r in range(4)], "x", 64)
    part_b = ring_scatter([line_b[r] for r in range(4)], "z", 64)
    grad_q = jnp.concatenate([part_a, part_b[:, : q_width - cut]], axis=1)
    grad_k = part_b[:, q_width - cut : q_width - cut + kv_width]
    grad_v = part_b[:, q_width - cut + kv_width :]

    grad_in = summed(by_block(after(d_qkv, both), w_qkv), "fs")

    going_home = tn(recv_table, out_planned).astype(bf16)
    returned = swap(going_home.reshape(count_dp, piece_rows, width)).reshape(count_rows, width)
    out_home = tn(send_table, returned).astype(bf16)

    return (out_home, grad_in, grad_q, grad_k, grad_v, wo_sum)


def solution(mesh):
    in_specs = (
        P("dp", "fs"),
        P("dp", "fs"),
        P("dp", "fs"),
        P("dp", "fs"),
        P("dp", "fs"),
        P("fs", "dp"),
        P(),
        P("dp", None),
    )
    out_specs = (
        P("dp", "fs"),
        P("dp", "fs"),
        P("dp", "fs"),
        P("dp", "fs"),
        P("dp", "fs"),
        P("fs", "dp"),
    )
    return jax.shard_map(local, mesh=mesh, in_specs=in_specs, out_specs=out_specs, check_vma=False)
```

```python
import jax
import jax.numpy as jnp
from jax import lax
from jax.experimental import pallas as pl
from jax.experimental.pallas import tpu as pltpu
from jax.sharding import PartitionSpec as P

HS = 128
NZ, NX, NC = 4, 4, 2
theta_base = 1000000.0
f32 = jnp.float32
bf16 = jnp.bfloat16


def angles(position, width):
    freq = theta_base ** (-(jnp.arange(width // 2, dtype=jnp.float32) * 2.0) / width)
    phase = position.astype(jnp.float32)[:, None] * freq[None, :]
    return (jnp.cos(phase), jnp.sin(phase))


def rotated(values, cosine, sine):
    return values * cosine + pltpu.roll(values, HS // 2, 1) * sine


def unrotated(values, cosine, sine):
    return values * cosine - pltpu.roll(values, HS // 2, 1) * sine


def mask_of(first_length, count_rows):
    row = lax.broadcasted_iota(jnp.int32, (count_rows, count_rows), 0)
    col = lax.broadcasted_iota(jnp.int32, (count_rows, count_rows), 1)
    return (col <= row) & ((row >= first_length) == (col >= first_length))


def probs_of(query, keys, allowed):
    scores = nt(query, keys) * (HS ** (-0.5))
    scores = jnp.where(allowed, scores, -1e30)
    expo = jnp.exp(scores - jnp.max(scores, axis=-1, keepdims=True))
    return expo / jnp.sum(expo, axis=-1, keepdims=True)


def nt(left, right):
    return lax.dot_general(left, right, (((1,), (1,)), ((), ())), preferred_element_type=f32)


def tn(left, right):
    return lax.dot_general(left, right, (((0,), (0,)), ((), ())), preferred_element_type=f32)


def nn(left, right):
    return jnp.dot(left, right, preferred_element_type=f32)


def accumulate(step, pieces, w_refs, acc):
    own, above, far_one, far_two, below = pieces
    half = far_one.shape[0]
    low = 0
    for w_ref in w_refs:
        cols = slice(low, low + w_ref.shape[1])
        low += w_ref.shape[1]

        @pl.when(step == 0)
        def _():
            acc[:, cols] = nn(own[...], w_ref[...])

        @pl.when(step == 1)
        def _():
            acc[:, cols] += nn(above[...], w_ref[...])

        @pl.when(step == 2)
        def _():
            acc[:half, cols] += nn(far_one[...], w_ref[...])
            acc[half:, cols] += nn(far_two[...], w_ref[...])

        @pl.when(step == 3)
        def _():
            acc[:, cols] += nn(below[...], w_ref[...])


def forward_kernel(info, own, above, far_one, far_two, below, wq_ref, wkv_ref, cos_ref, sin_ref,
                   q_ref, k_ref, v_ref, flat_ref, acc):
    step = pl.program_id(0)
    accumulate(step, (own, above, far_one, far_two, below), (wq_ref, wkv_ref), acc)
    count_rows, q_width = q_ref.shape

    @pl.when(step == 3)
    def _():
        cosine, sine = cos_ref[...], sin_ref[...]
        keys = rotated(acc[:, q_width : q_width + HS], cosine, sine).astype(bf16)
        values = acc[:, q_width + HS :].astype(bf16)
        k_ref[...] = keys
        v_ref[...] = values
        allowed = mask_of(info[1], count_rows)
        for head in range(q_width // HS):
            cols = slice(head * HS, (head + 1) * HS)
            query = rotated(acc[:, cols], cosine, sine).astype(bf16)
            q_ref[:, cols] = query
            low = probs_of(query, keys, allowed).astype(bf16)
            flat_ref[:, cols] = nn(low, values).astype(bf16)


def backward_kernel(info, own, above, far_one, far_two, below, w_ref, cos_ref, sin_ref,
                    q_ref, k_ref, v_ref, flat_ref, grad_ref, acc):
    step = pl.program_id(0)
    accumulate(step, (own, above, far_one, far_two, below), (w_ref,), acc)
    count_rows, q_width = q_ref.shape

    @pl.when(step == 3)
    def _():
        cosine, sine = cos_ref[...], sin_ref[...]
        keys, values = k_ref[...], v_ref[...]
        allowed = mask_of(info[1], count_rows)
        d_keys = jnp.zeros((count_rows, HS), f32)
        d_values = jnp.zeros((count_rows, HS), f32)
        for head in range(q_width // HS):
            cols = slice(head * HS, (head + 1) * HS)
            query = q_ref[:, cols]
            d_att = acc[:, cols].astype(bf16)
            probs = probs_of(query, keys, allowed)
            delta = jnp.sum(
                d_att.astype(f32) * flat_ref[:, cols].astype(f32), axis=-1, keepdims=True
            )
            d_probs = nt(d_att, values)
            d_scores = (probs * (d_probs - delta) * (HS ** (-0.5))).astype(bf16)
            d_values += tn(probs.astype(bf16), d_att)
            d_keys += tn(d_scores, query)
            grad_ref[:, cols] = unrotated(nn(d_scores, keys), cosine, sine).astype(bf16)
        grad_ref[:, q_width : q_width + HS] = unrotated(d_keys, cosine, sine).astype(bf16)
        grad_ref[:, q_width + HS :] = d_values.astype(bf16)


def blocks_kernel(left_ref, w_ref, out_ref):
    out_ref[0] = nt(left_ref[...], w_ref[...]).astype(bf16)


def pair_kernel(left_ref, right_ref, came_a, came_b, *outs):
    lines, shard = came_a.shape[0] // 4, came_a.shape[0] // 16
    cut = came_a.shape[1]
    for at in range(4):
        rows = slice(at * lines, (at + 1) * lines)
        here = nn(left_ref[rows], right_ref[...])
        sum_a = (here[:, :cut] + came_a[rows].astype(f32)).astype(bf16)
        sum_b = (here[:, cut:] + came_b[rows].astype(f32)).astype(bf16)
        if at == 2:
            outs[2][...] = sum_a[: lines // 2].reshape(outs[2].shape)
            outs[3][...] = sum_a[lines // 2 :].reshape(outs[3].shape)
        else:
            place = {0: 0, 1: 1, 3: 4}[at]
            outs[place][...] = sum_a.reshape(outs[place].shape)
        for to in range(4):
            part = sum_b[to * shard : (to + 1) * shard]
            if to == 2:
                outs[7 if at < 2 else 8][at % 2] = part
            else:
                outs[{0: 5, 1: 6, 3: 9}[to]][at] = part


def join_kernel(one_a, three_a, down_a, up_a, one_b, three_b, down_b, up_b, *outs):
    for index, (one, three, down, up) in enumerate(
        ((one_a, three_a, down_a, up_a), (one_b, three_b, down_b, up_b))
    ):
        half = down.shape[0]
        to_one, to_three = outs[2 * index : 2 * index + 2]
        to_one[:half] = (one[:half].astype(f32) + down[...].astype(f32)).astype(bf16)
        to_one[half:] = one[half:]
        to_three[:half] = three[:half]
        to_three[half:] = (three[half:].astype(f32) + up[...].astype(f32)).astype(bf16)


def spread_kernel(info, left_ref, wq_ref, wkv_ref, own, one, far_one, far_two, three):
    step = pl.program_id(0)
    half = far_one.shape[0]
    q_width = wq_ref.shape[1]
    block = nt(left_ref[:, :q_width], wq_ref[...]) + nt(left_ref[:, q_width:], wkv_ref[...])
    block = block.astype(bf16)

    @pl.when(step == 0)
    def _():
        own[...] = block

    @pl.when(step == 1)
    def _():
        one[...] = block

    @pl.when(step == 2)
    def _():
        far_one[...] = block[:half]
        far_two[...] = block[half:]

    @pl.when(step == 3)
    def _():
        three[...] = block


def grad_out_kernel(info, own, above, far_one, far_two, below, flat_ref, out_ref):
    step = pl.program_id(0)
    half = far_one.shape[0]

    @pl.when(step == 0)
    def _():
        out_ref[...] = tn(own[...], flat_ref[...]).astype(bf16)

    @pl.when(step == 1)
    def _():
        out_ref[...] = tn(above[...], flat_ref[...]).astype(bf16)

    @pl.when(step == 2)
    def _():
        total = tn(far_one[...], flat_ref[:half]) + tn(far_two[...], flat_ref[half:])
        out_ref[...] = total.astype(bf16)

    @pl.when(step == 3)
    def _():
        out_ref[...] = tn(below[...], flat_ref[...]).astype(bf16)


def transpose_kernel(info, own, above, far_one, far_two, below, out_ref):
    step = pl.program_id(0)
    shard = out_ref.shape[3]

    def put(piece):
        turned = piece.T
        for at_x in range(4):
            for at_c in range(2):
                start = (at_x * 2 + at_c) * shard
                out_ref[(at_c + info[4]) % 2, 0, (at_x + 4 - info[3]) % 4] = (
                    turned[start : start + shard]
                )

    @pl.when(step == 0)
    def _():
        put(own[...])

    @pl.when(step == 1)
    def _():
        put(above[...])

    @pl.when(step == 2)
    def _():
        put(jnp.concatenate([far_one[...], far_two[...]], axis=0))

    @pl.when(step == 3)
    def _():
        put(below[...])


def fixed(array):
    zeros = (0,) * array.ndim
    return pl.BlockSpec(array.shape, lambda *_: zeros)


PARAMS = dict(compiler_params=pltpu.CompilerParams(vmem_limit_bytes=48 * 1024 * 1024))


def shape_of(*dims):
    return jax.ShapeDtypeStruct(dims, bf16)


def by_piece(kernel, info, operands, w, outs, out_specs, scratch):
    specs = [fixed(operand) for operand in operands]
    at = min(5, len(operands))

    def block_of(array, cols, place):
        return pl.BlockSpec((array.shape[0] // 4, cols), lambda k, s: ((s[0] + k) % 4, place))

    specs = specs[:at] + [block_of(*item) for item in w] + specs[at:]
    operands = operands[:at] + [item[0] for item in w] + operands[at:]
    return pl.pallas_call(
        kernel,
        out_shape=outs,
        grid_spec=pltpu.PrefetchScalarGridSpec(
            num_scalar_prefetch=1, grid=(4,), in_specs=specs, out_specs=out_specs,
            scratch_shapes=scratch,
        ),
        **PARAMS,
    )(info, *operands)


def by_block(left, w, cols, place):
    block = w.shape[0] // 4
    return pl.pallas_call(
        blocks_kernel,
        out_shape=shape_of(4, left.shape[0], block),
        grid=(4,),
        in_specs=[fixed(left), pl.BlockSpec((block, cols), lambda k: (k, place))],
        out_specs=pl.BlockSpec((1, left.shape[0], block), lambda k: (k, 0, 0)),
        **PARAMS,
    )(left, w)


def dp_index(z, x, c):
    return ((z % NZ) * NX + x % NX) * NC + c % NC


DP_ALL = [(z, x, c) for z in range(NZ) for x in range(NX) for c in range(NC)]
PERMS = {
    "z": lambda s: [(dp_index(z, x, c), dp_index(z + s, x, c)) for z, x, c in DP_ALL],
    "x": lambda s: [(dp_index(z, x, c), dp_index(z, x + s, c)) for z, x, c in DP_ALL],
    "core": lambda s: [(dp_index(z, x, c), dp_index(z, x, c + s)) for z, x, c in DP_ALL],
}


def shift(values, axis, step):
    if axis == "fs":
        return lax.ppermute(values, "fs", [(i, (i + step) % 4) for i in range(4)])
    return lax.ppermute(values, "dp", PERMS[axis](step))


def add(*terms):
    return sum([term.astype(f32) for term in terms]).astype(bf16)


def ring_first(own, axis):
    return shift(own, axis, 1), shift(own, axis, -1)


def ring_rest(own, first, axis):
    below, above = first
    half = own.shape[0] // 2
    return [own, above, shift(below[:half], axis, 1), shift(above[half:], axis, -1), below]


def together(*values):
    return lax.optimization_barrier(values)


def scatter_start(pieces, axis):
    return shift(pieces[2], axis, 1), shift(pieces[3], axis, -1)


def direct(pieces, axis):
    return [shift(pieces[r], axis, r) for r in (1, 2, 3)]


def after(values, first):
    return lax.optimization_barrier((values, first))[0]


def local(tokens, cotangent, w_query, w_key, w_value, w_out, route, doc_lengths):
    count_dp = lax.axis_size("dp")
    my_index = lax.axis_index("dp")
    my_fs = lax.axis_index("fs")
    my_z, my_x, my_c = my_index // 8, (my_index // 2) % 4, my_index % 2
    count_rows, width = tokens.shape
    piece_rows = count_rows // count_dp
    shard = w_query.shape[0]
    q_width, kv_width = w_query.shape[1], w_key.shape[1]

    w_all = lax.all_gather(
        jnp.concatenate([w_query, w_out.T, w_key, w_value], axis=1), "dp", axis=0, tiled=True
    )
    line_ids = jnp.arange(count_rows, dtype=jnp.int32)
    own_route = lax.dynamic_slice_in_dim(route, my_index * count_rows, count_rows)
    send_rank = jnp.sum((own_route[None, :] < own_route[:, None]).astype(jnp.int32), axis=1)
    send_table = (send_rank[None, :] == line_ids[:, None]).astype(bf16)

    planned = my_index * count_rows + line_ids
    home_block = jnp.arange(route.shape[0], dtype=jnp.int32) // count_rows
    source = jnp.sum(jnp.where(route[None, :] == planned[:, None], home_block[None, :], 0), axis=1)
    earlier = (source[None, :] == source[:, None]) & (line_ids[None, :] < line_ids[:, None])
    buffer_row = source * piece_rows + jnp.sum(earlier.astype(jnp.int32), axis=1)
    recv_table = (buffer_row[:, None] == line_ids[None, :]).astype(bf16)

    def outbound(values):
        moved = nn(send_table, values).astype(bf16)
        return moved.reshape(count_dp, piece_rows, values.shape[1])

    def inbound(values):
        return nn(recv_table, values.reshape(count_rows, values.shape[2])).astype(bf16)

    def swap(values):
        return lax.all_to_all(values, "dp", split_axis=0, concat_axis=0, tiled=True)

    def exchanged(blocks):
        return lax.all_to_all(blocks, "fs", split_axis=0, concat_axis=0, tiled=True)

    def total(came):
        return add(*[came[r] for r in range(4)])

    first_length = doc_lengths[0, 0]
    position = line_ids - jnp.where(line_ids >= first_length, first_length, 0)
    cosine, sine = angles(position, HS)
    cosine = jnp.concatenate([cosine, cosine], axis=1)
    sine = jnp.concatenate([-sine, sine], axis=1)
    info = jnp.stack([my_fs, first_length, my_z, my_x, my_c]).astype(jnp.int32)

    x_own = inbound(swap(outbound(tokens)))
    x_first = ring_first(x_own, "fs")
    c_own = inbound(swap(after(outbound(cotangent), x_own)))
    x_pieces = ring_rest(x_own, x_first, "fs")
    c_pieces = ring_rest(c_own, ring_first(c_own, "fs"), "fs")

    x_turned = by_piece(
        transpose_kernel, info, x_pieces, [],
        shape_of(2, 4, 4, shard, count_rows),
        pl.BlockSpec((2, 1, 4, shard, count_rows), lambda k, s: (0, (s[0] + k + 4 - s[2]) % 4, 0, 0, 0)),
        [],
    )
    own_t, other_t = [x_turned[i].reshape(16 * shard, count_rows) for i in range(2)]
    w_all, own_t, other_t, c_pieces = together(w_all, own_t, other_t, c_pieces)
    w_qkv = [(w_all, q_width, 0), (w_all, 2 * kv_width, q_width // kv_width)]
    w_out_t = [(w_all, q_width, 1)]

    rows_of = lambda cols: pl.BlockSpec((count_rows, cols), lambda *_: (0, 0))
    query, keys, values, flat = by_piece(
        forward_kernel, info, x_pieces + [cosine, sine], w_qkv,
        (shape_of(count_rows, q_width), shape_of(count_rows, kv_width),
         shape_of(count_rows, kv_width), shape_of(count_rows, q_width)),
        (rows_of(q_width), rows_of(kv_width), rows_of(kv_width), rows_of(q_width)),
        [pltpu.VMEM((count_rows, q_width + 2 * kv_width), f32)],
    )

    grad_out_part = by_piece(
        grad_out_kernel, info, c_pieces + [flat], [],
        shape_of(4 * width, q_width),
        pl.BlockSpec((width, q_width), lambda k, s: ((s[0] + k) % 4, 0)),
        [],
    )
    wo_sum = lax.psum_scatter(grad_out_part, "dp", scatter_dimension=0, tiled=True).T

    d_qkv = by_piece(
        backward_kernel, info,
        after(c_pieces, grad_out_part) + [cosine, sine, query, keys, values, flat], w_out_t,
        shape_of(count_rows, q_width + 2 * kv_width), rows_of(q_width + 2 * kv_width),
        [pltpu.VMEM((count_rows, q_width), f32)],
    )

    cut = 5 * HS
    cols = (d_qkv[:, :cut], d_qkv[:, cut:])
    there = [nn(other_t, part).astype(bf16) for part in cols]
    came = [shift(block, "core", 1) for block in there]
    head_blocks = by_block(after(flat, there), *w_out_t[0])
    out_came = exchanged(head_blocks)

    whole_array = lambda *arrays: [fixed(array) for array in arrays]
    shapes = []
    for part in cols:
        block = (4, shard, part.shape[1])
        shapes += [block, block, (2,) + block[1:], (2,) + block[1:], block]
    shapes = [shape_of(*dims) for dims in shapes]
    pair_in = (after(own_t, head_blocks), d_qkv, *came)
    pieces = pl.pallas_call(
        pair_kernel, out_shape=shapes, in_specs=whole_array(*pair_in),
        out_specs=whole_array(*shapes), grid=(1,), **PARAMS,
    )(*pair_in)
    pieces_a, pieces_b = pieces[:5], pieces[5:]
    step_a, step_b = scatter_start(pieces_a, "z"), scatter_start(pieces_b, "x")

    grad_blocks = by_piece(
        spread_kernel, info, [d_qkv], w_qkv,
        [shape_of(count_rows, width)] * 2 + [shape_of(count_rows // 2, width)] * 2
        + [shape_of(count_rows, width)],
        [rows_of(width)] * 2
        + [pl.BlockSpec((count_rows // 2, width), lambda *_: (0, 0))] * 2 + [rows_of(width)],
        [],
    )
    step_a, step_b, grad_blocks = together(step_a, step_b, grad_blocks)
    join_in = (pieces_a[1], pieces_a[4], *step_a, pieces_b[1], pieces_b[4], *step_b)
    join_out = [shapes[0]] * 2 + [shapes[5]] * 2
    one_a, three_a, one_b, three_b = pl.pallas_call(
        join_kernel, out_shape=join_out, in_specs=whole_array(*join_in),
        out_specs=whole_array(*join_out), grid=(1,), **PARAMS,
    )(*join_in)
    step_a = (shift(one_a, "z", 1), shift(three_a, "z", -1))
    step_b = (shift(one_b, "x", 1), shift(three_b, "x", -1))
    step_g = scatter_start(grad_blocks, "fs")
    going_home = tn(recv_table, total(after(out_came, one_a))).astype(bf16)
    returned = swap(going_home.reshape(count_dp, piece_rows, width))
    step_a, step_b, step_g = together(step_a, step_b, step_g)
    line_a, line_b = add(pieces_a[0], *step_a), add(pieces_b[0], *step_b)
    half = count_rows // 2
    one_g = jnp.concatenate([add(grad_blocks[1][:half], step_g[0]), grad_blocks[1][half:]], axis=0)
    three_g = jnp.concatenate(
        [grad_blocks[4][:half], add(grad_blocks[4][half:], step_g[1])], axis=0
    )
    grad_in = add(grad_blocks[0], shift(one_g, "fs", 1), shift(three_g, "fs", -1))
    returned = after(returned, (line_a, line_b))
    out_home = tn(send_table, returned.reshape(count_rows, width)).astype(bf16)
    part_a = add(line_a[0], *direct(line_a, "x"))
    part_b = add(line_b[0], *direct(line_b, "z"))
    grad_q = jnp.concatenate([part_a, part_b[:, : q_width - cut]], axis=1)
    grad_k = part_b[:, q_width - cut : q_width - cut + kv_width]
    grad_v = part_b[:, q_width - cut + kv_width :]

    return (out_home, grad_in, grad_q, grad_k, grad_v, wo_sum)


def solution(mesh):
    in_specs = (
        P("dp", "fs"),
        P("dp", "fs"),
        P("dp", "fs"),
        P("dp", "fs"),
        P("dp", "fs"),
        P("fs", "dp"),
        P(),
        P("dp", None),
    )
    out_specs = (
        P("dp", "fs"),
        P("dp", "fs"),
        P("dp", "fs"),
        P("dp", "fs"),
        P("dp", "fs"),
        P("fs", "dp"),
    )
    return jax.shard_map(local, mesh=mesh, in_specs=in_specs, out_specs=out_specs, check_vma=False)
```

```python
import jax
import jax.numpy as jnp
from jax import lax
from jax.experimental import pallas as pl
from jax.experimental.pallas import tpu as pltpu
from jax.sharding import PartitionSpec as P

HS = 128
NZ, NX, NC = 4, 4, 2
theta_base = 1000000.0
f32 = jnp.float32
bf16 = jnp.bfloat16


def angles(position, width):
    freq = theta_base ** (-(jnp.arange(width // 2, dtype=jnp.float32) * 2.0) / width)
    phase = position.astype(jnp.float32)[:, None] * freq[None, :]
    return (jnp.cos(phase), jnp.sin(phase))


def rotated(values, cosine, sine):
    return values * cosine + pltpu.roll(values, HS // 2, 1) * sine


def unrotated(values, cosine, sine):
    return values * cosine - pltpu.roll(values, HS // 2, 1) * sine


def mask_of(first_length, count_rows):
    row = lax.broadcasted_iota(jnp.int32, (count_rows, count_rows), 0)
    col = lax.broadcasted_iota(jnp.int32, (count_rows, count_rows), 1)
    return (col <= row) & ((row >= first_length) == (col >= first_length))


def probs_of(query, keys, allowed):
    scores = nt(query, keys) * (HS ** (-0.5))
    scores = jnp.where(allowed, scores, -1e30)
    expo = jnp.exp(scores - jnp.max(scores, axis=-1, keepdims=True))
    return expo / jnp.sum(expo, axis=-1, keepdims=True)


def nt(left, right):
    return lax.dot_general(left, right, (((1,), (1,)), ((), ())), preferred_element_type=f32)


def tn(left, right):
    return lax.dot_general(left, right, (((0,), (0,)), ((), ())), preferred_element_type=f32)


def nn(left, right):
    return jnp.dot(left, right, preferred_element_type=f32)


def accumulate(step, first, pieces, w_refs, acc):
    own, above, far_one, far_two, below = pieces
    half = far_one.shape[0]
    low = 0
    for w_ref in w_refs:
        cols = slice(low, low + w_ref.shape[1])
        low += w_ref.shape[1]

        @pl.when(step == first)
        def _():
            acc[:, cols] = nn(own[...], w_ref[...])

        @pl.when(step == first + 1)
        def _():
            acc[:, cols] += nn(above[...], w_ref[...])

        @pl.when(step == first + 2)
        def _():
            acc[:half, cols] += nn(far_one[...], w_ref[...])
            acc[half:, cols] += nn(far_two[...], w_ref[...])

        @pl.when(step == first + 3)
        def _():
            acc[:, cols] += nn(below[...], w_ref[...])


def attend_kernel(info, *refs):
    x_pieces, c_pieces, refs = refs[:5], refs[5:10], refs[10:]
    wq_ref, wkv_ref, wo_ref, cos_ref, sin_ref, flat_ref, grad_ref, acc, acc_att = refs
    step = pl.program_id(0)
    accumulate(step, 0, x_pieces, (wq_ref, wkv_ref), acc)
    accumulate(step, 4, c_pieces, (wo_ref,), acc_att)
    count_rows, q_width = flat_ref.shape
    scale = HS ** (-0.5)

    @pl.when(step == 7)
    def _():
        cosine, sine = cos_ref[...], sin_ref[...]
        keys = rotated(acc[:, q_width : q_width + HS], cosine, sine).astype(bf16)
        values = acc[:, q_width + HS :].astype(bf16)
        allowed = mask_of(info[1], count_rows)
        d_keys = jnp.zeros((count_rows, HS), f32)
        d_values = jnp.zeros((count_rows, HS), f32)
        for head in range(q_width // HS):
            cols = slice(head * HS, (head + 1) * HS)
            query = rotated(acc[:, cols], cosine, sine).astype(bf16)
            d_att = acc_att[:, cols].astype(bf16)
            probs = probs_of(query, keys, allowed)
            low = probs.astype(bf16)
            attended = nn(low, values).astype(bf16)
            flat_ref[:, cols] = attended
            delta = jnp.sum(d_att.astype(f32) * attended.astype(f32), axis=-1, keepdims=True)
            d_scores = (probs * (nt(d_att, values) - delta) * scale).astype(bf16)
            d_values += tn(low, d_att)
            d_keys += tn(d_scores, query)
            grad_ref[:, cols] = unrotated(nn(d_scores, keys), cosine, sine).astype(bf16)
        grad_ref[:, q_width : q_width + HS] = unrotated(d_keys, cosine, sine).astype(bf16)
        grad_ref[:, q_width + HS :] = d_values.astype(bf16)


def blocks_kernel(left_ref, *refs):
    low, block = 0, 0.0
    for w_ref in refs[:-1]:
        high = low + w_ref.shape[1]
        block = block + nt(left_ref[:, low:high], w_ref[...])
        low = high
    refs[-1][0] = block.astype(bf16)


def pair_kernel(left_ref, right_ref, came_a, came_b, *outs):
    lines, shard = came_a.shape[0] // 4, came_a.shape[0] // 16
    cut = came_a.shape[1]
    for at in range(4):
        rows = slice(at * lines, (at + 1) * lines)
        here = nn(left_ref[rows], right_ref[...])
        sum_a = (here[:, :cut] + came_a[rows].astype(f32)).astype(bf16)
        sum_b = (here[:, cut:] + came_b[rows].astype(f32)).astype(bf16)
        if at == 2:
            outs[2][...] = sum_a[: lines // 2].reshape(outs[2].shape)
            outs[3][...] = sum_a[lines // 2 :].reshape(outs[3].shape)
        else:
            place = {0: 0, 1: 1, 3: 4}[at]
            outs[place][...] = sum_a.reshape(outs[place].shape)
        for to in range(4):
            part = sum_b[to * shard : (to + 1) * shard]
            if to == 2:
                outs[7 if at < 2 else 8][at % 2] = part
            else:
                outs[{0: 5, 1: 6, 3: 9}[to]][at] = part


def join_kernel(one_a, three_a, down_a, up_a, one_b, three_b, down_b, up_b, *outs):
    for index, (one, three, down, up) in enumerate(
        ((one_a, three_a, down_a, up_a), (one_b, three_b, down_b, up_b))
    ):
        half = down.shape[0]
        to_one, to_three = outs[2 * index : 2 * index + 2]
        to_one[:half] = (one[:half].astype(f32) + down[...].astype(f32)).astype(bf16)
        to_one[half:] = one[half:]
        to_three[:half] = three[:half]
        to_three[half:] = (three[half:].astype(f32) + up[...].astype(f32)).astype(bf16)


def spread_kernel(info, left_ref, wq_ref, wkv_ref, own, one, far_one, far_two, three):
    step = pl.program_id(0)
    half = far_one.shape[0]
    q_width = wq_ref.shape[1]
    block = nt(left_ref[:, :q_width], wq_ref[...]) + nt(left_ref[:, q_width:], wkv_ref[...])
    block = block.astype(bf16)

    @pl.when(step == 0)
    def _():
        own[...] = block

    @pl.when(step == 1)
    def _():
        one[...] = block

    @pl.when(step == 2)
    def _():
        far_one[...] = block[:half]
        far_two[...] = block[half:]

    @pl.when(step == 3)
    def _():
        three[...] = block


def grad_out_kernel(info, own, above, far_one, far_two, below, flat_ref, out_ref):
    step = pl.program_id(0)
    half = far_one.shape[0]

    @pl.when(step == 0)
    def _():
        out_ref[...] = tn(own[...], flat_ref[...]).astype(bf16)

    @pl.when(step == 1)
    def _():
        out_ref[...] = tn(above[...], flat_ref[...]).astype(bf16)

    @pl.when(step == 2)
    def _():
        total = tn(far_one[...], flat_ref[:half]) + tn(far_two[...], flat_ref[half:])
        out_ref[...] = total.astype(bf16)

    @pl.when(step == 3)
    def _():
        out_ref[...] = tn(below[...], flat_ref[...]).astype(bf16)


def transpose_kernel(info, own, above, far_one, far_two, below, out_ref):
    step = pl.program_id(0)
    shard = out_ref.shape[3]

    def put(piece):
        turned = piece.T
        for at_x in range(4):
            for at_c in range(2):
                start = (at_x * 2 + at_c) * shard
                out_ref[(at_c + info[4]) % 2, 0, (at_x + 4 - info[3]) % 4] = (
                    turned[start : start + shard]
                )

    @pl.when(step == 0)
    def _():
        put(own[...])

    @pl.when(step == 1)
    def _():
        put(above[...])

    @pl.when(step == 2)
    def _():
        put(jnp.concatenate([far_one[...], far_two[...]], axis=0))

    @pl.when(step == 3)
    def _():
        put(below[...])


def fixed(array):
    zeros = (0,) * array.ndim
    return pl.BlockSpec(array.shape, lambda *_: zeros)


PARAMS = dict(compiler_params=pltpu.CompilerParams(vmem_limit_bytes=48 * 1024 * 1024))


def shape_of(*dims):
    return jax.ShapeDtypeStruct(dims, bf16)


def by_piece(kernel, info, operands, w, outs, out_specs, scratch):
    specs = [fixed(operand) for operand in operands]
    at = min(5, len(operands))

    def block_of(array, cols, place):
        return pl.BlockSpec((array.shape[0] // 4, cols), lambda k, s: ((s[0] + k) % 4, place))

    specs = specs[:at] + [block_of(*item) for item in w] + specs[at:]
    operands = operands[:at] + [item[0] for item in w] + operands[at:]
    return pl.pallas_call(
        kernel,
        out_shape=outs,
        grid_spec=pltpu.PrefetchScalarGridSpec(
            num_scalar_prefetch=1, grid=(4,), in_specs=specs, out_specs=out_specs,
            scratch_shapes=scratch,
        ),
        **PARAMS,
    )(info, *operands)


def by_block(left, w):
    block = w[0][0].shape[0] // 4

    def block_of(cols, place):
        return pl.BlockSpec((block, cols), lambda k: (k, place))

    return pl.pallas_call(
        blocks_kernel,
        out_shape=shape_of(4, left.shape[0], block),
        grid=(4,),
        in_specs=[fixed(left)] + [block_of(*item[1:]) for item in w],
        out_specs=pl.BlockSpec((1, left.shape[0], block), lambda k: (k, 0, 0)),
        **PARAMS,
    )(left, *[item[0] for item in w])


def dp_index(z, x, c):
    return ((z % NZ) * NX + x % NX) * NC + c % NC


DP_ALL = [(z, x, c) for z in range(NZ) for x in range(NX) for c in range(NC)]
PERMS = {
    "z": lambda s: [(dp_index(z, x, c), dp_index(z + s, x, c)) for z, x, c in DP_ALL],
    "x": lambda s: [(dp_index(z, x, c), dp_index(z, x + s, c)) for z, x, c in DP_ALL],
    "core": lambda s: [(dp_index(z, x, c), dp_index(z, x, c + s)) for z, x, c in DP_ALL],
}


def shift(values, axis, step):
    if axis == "fs":
        return lax.ppermute(values, "fs", [(i, (i + step) % 4) for i in range(4)])
    return lax.ppermute(values, "dp", PERMS[axis](step))


def add(*terms):
    return sum([term.astype(f32) for term in terms]).astype(bf16)


def ring_first(own, axis):
    return shift(own, axis, 1), shift(own, axis, -1)


def ring_rest(own, first, axis):
    below, above = first
    half = own.shape[0] // 2
    return [own, above, shift(below[:half], axis, 1), shift(above[half:], axis, -1), below]


def together(*values):
    return lax.optimization_barrier(values)


def scatter_start(pieces, axis):
    return shift(pieces[2], axis, 1), shift(pieces[3], axis, -1)


def direct(pieces, axis):
    return [shift(pieces[r], axis, r) for r in (1, 2, 3)]


def after(values, first):
    return lax.optimization_barrier((values, first))[0]


def local(tokens, cotangent, w_query, w_key, w_value, w_out, route, doc_lengths):
    count_dp = lax.axis_size("dp")
    my_index = lax.axis_index("dp")
    my_fs = lax.axis_index("fs")
    my_z, my_x, my_c = my_index // 8, (my_index // 2) % 4, my_index % 2
    count_rows, width = tokens.shape
    piece_rows = count_rows // count_dp
    shard = w_query.shape[0]
    q_width, kv_width = w_query.shape[1], w_key.shape[1]

    w_all = lax.all_gather(
        jnp.concatenate([w_query, w_out.T, w_key, w_value], axis=1), "dp", axis=0, tiled=True
    )
    line_ids = jnp.arange(count_rows, dtype=jnp.int32)
    own_route = lax.dynamic_slice_in_dim(route, my_index * count_rows, count_rows)
    send_rank = jnp.sum((own_route[None, :] < own_route[:, None]).astype(jnp.int32), axis=1)
    send_table = (send_rank[None, :] == line_ids[:, None]).astype(bf16)

    planned = my_index * count_rows + line_ids
    home_block = jnp.arange(route.shape[0], dtype=jnp.int32) // count_rows
    source = jnp.sum(jnp.where(route[None, :] == planned[:, None], home_block[None, :], 0), axis=1)
    earlier = (source[None, :] == source[:, None]) & (line_ids[None, :] < line_ids[:, None])
    buffer_row = source * piece_rows + jnp.sum(earlier.astype(jnp.int32), axis=1)
    recv_table = (buffer_row[:, None] == line_ids[None, :]).astype(bf16)

    def outbound(values):
        moved = nn(send_table, values).astype(bf16)
        return moved.reshape(count_dp, piece_rows, values.shape[1])

    def inbound(values):
        return nn(recv_table, values.reshape(count_rows, values.shape[2])).astype(bf16)

    def swap(values):
        return lax.all_to_all(values, "dp", split_axis=0, concat_axis=0, tiled=True)

    def exchanged(blocks):
        return lax.all_to_all(blocks, "fs", split_axis=0, concat_axis=0, tiled=True)

    def total(came):
        return add(*[came[r] for r in range(4)])

    first_length = doc_lengths[0, 0]
    position = line_ids - jnp.where(line_ids >= first_length, first_length, 0)
    cosine, sine = angles(position, HS)
    cosine = jnp.concatenate([cosine, cosine], axis=1)
    sine = jnp.concatenate([-sine, sine], axis=1)
    info = jnp.stack([my_fs, first_length, my_z, my_x, my_c]).astype(jnp.int32)

    x_own = inbound(swap(outbound(tokens)))
    x_first = ring_first(x_own, "fs")
    c_own = inbound(swap(after(outbound(cotangent), x_own)))
    x_pieces = ring_rest(x_own, x_first, "fs")
    c_pieces = ring_rest(c_own, ring_first(c_own, "fs"), "fs")

    x_turned = by_piece(
        transpose_kernel, info, x_pieces, [],
        shape_of(2, 4, 4, shard, count_rows),
        pl.BlockSpec((2, 1, 4, shard, count_rows), lambda k, s: (0, (s[0] + k + 4 - s[2]) % 4, 0, 0, 0)),
        [],
    )
    own_t, other_t = [x_turned[i].reshape(16 * shard, count_rows) for i in range(2)]
    w_all, own_t, other_t, c_pieces = together(w_all, own_t, other_t, c_pieces)
    w_qkv = [(w_all, q_width, 0), (w_all, 2 * kv_width, q_width // kv_width)]
    w_out_t = [(w_all, q_width, 1)]

    rows_of = lambda cols: pl.BlockSpec((count_rows, cols), lambda *_: (0, 0))
    def w_block(item, first):
        array, cols, place = item
        return pl.BlockSpec(
            (array.shape[0] // 4, cols),
            lambda k, s: ((s[0] + jnp.clip(k - first, 0, 3)) % 4, place),
        )

    total_width = q_width + 2 * kv_width
    pieces = list(x_pieces) + list(c_pieces)
    flat, d_qkv = pl.pallas_call(
        attend_kernel,
        out_shape=(shape_of(count_rows, q_width), shape_of(count_rows, total_width)),
        grid_spec=pltpu.PrefetchScalarGridSpec(
            num_scalar_prefetch=1, grid=(8,),
            in_specs=[fixed(piece) for piece in pieces]
            + [w_block(w_qkv[0], 0), w_block(w_qkv[1], 0), w_block(w_out_t[0], 4)]
            + [fixed(cosine), fixed(sine)],
            out_specs=(rows_of(q_width), rows_of(total_width)),
            scratch_shapes=[
                pltpu.VMEM((count_rows, total_width), f32), pltpu.VMEM((count_rows, q_width), f32),
            ],
        ),
        **PARAMS,
    )(info, *pieces, w_all, w_all, w_all, cosine, sine)

    cut = 5 * HS
    cols = (d_qkv[:, :cut], d_qkv[:, cut:])
    there = [nn(other_t, part).astype(bf16) for part in cols]
    came = [shift(block, "core", 1) for block in there]
    grad_out_part = by_piece(
        grad_out_kernel, info, after(c_pieces, there) + [flat], [],
        shape_of(4 * width, q_width),
        pl.BlockSpec((width, q_width), lambda k, s: ((s[0] + k) % 4, 0)),
        [],
    )
    wo_sum = lax.psum_scatter(grad_out_part, "dp", scatter_dimension=0, tiled=True).T

    whole_array = lambda *arrays: [fixed(array) for array in arrays]
    shapes = []
    for part in cols:
        block = (4, shard, part.shape[1])
        shapes += [block, block, (2,) + block[1:], (2,) + block[1:], block]
    shapes = [shape_of(*dims) for dims in shapes]
    head_blocks = by_block(after(flat, grad_out_part), w_out_t)
    out_came = exchanged(head_blocks)
    pair_in = (after(own_t, head_blocks), d_qkv, *came)
    pieces = pl.pallas_call(
        pair_kernel, out_shape=shapes, in_specs=whole_array(*pair_in),
        out_specs=whole_array(*shapes), grid=(1,), **PARAMS,
    )(*pair_in)
    pieces_a, pieces_b = pieces[:5], pieces[5:]
    step_a, step_b = scatter_start(pieces_a, "z"), scatter_start(pieces_b, "x")

    grad_blocks = by_piece(
        spread_kernel, info, [after(d_qkv, pieces)], w_qkv,
        [shape_of(count_rows, width)] * 2 + [shape_of(count_rows // 2, width)] * 2
        + [shape_of(count_rows, width)],
        [rows_of(width)] * 2
        + [pl.BlockSpec((count_rows // 2, width), lambda *_: (0, 0))] * 2 + [rows_of(width)],
        [],
    )
    step_a, step_b, grad_blocks = together(step_a, step_b, grad_blocks)
    join_in = (pieces_a[1], pieces_a[4], *step_a, pieces_b[1], pieces_b[4], *step_b)
    join_out = [shapes[0]] * 2 + [shapes[5]] * 2
    one_a, three_a, one_b, three_b = pl.pallas_call(
        join_kernel, out_shape=join_out, in_specs=whole_array(*join_in),
        out_specs=whole_array(*join_out), grid=(1,), **PARAMS,
    )(*join_in)
    step_a = (shift(one_a, "z", 1), shift(three_a, "z", -1))
    step_b = (shift(one_b, "x", 1), shift(three_b, "x", -1))
    step_a, step_b, grad_blocks = together(step_a, step_b, grad_blocks)
    step_g = scatter_start(grad_blocks, "fs")
    line_a, line_b = add(pieces_a[0], *step_a), add(pieces_b[0], *step_b)
    out_came, *step_g = together(out_came, *step_g, line_a)[:3]
    going_home = tn(recv_table, total(out_came)).astype(bf16)
    returned = swap(going_home.reshape(count_dp, piece_rows, width))
    half = count_rows // 2
    one_g = jnp.concatenate([add(grad_blocks[1][:half], step_g[0]), grad_blocks[1][half:]], axis=0)
    three_g = jnp.concatenate(
        [grad_blocks[4][:half], add(grad_blocks[4][half:], step_g[1])], axis=0
    )
    step_g = (shift(one_g, "fs", 1), shift(three_g, "fs", -1))
    returned, step_g = together(returned, step_g)
    grad_in = add(grad_blocks[0], *step_g)
    out_home = tn(send_table, returned.reshape(count_rows, width)).astype(bf16)
    part_a = add(line_a[0], *direct(line_a, "x"))
    part_b = add(line_b[0], *direct(line_b, "z"))
    grad_q = jnp.concatenate([part_a, part_b[:, : q_width - cut]], axis=1)
    grad_k = part_b[:, q_width - cut : q_width - cut + kv_width]
    grad_v = part_b[:, q_width - cut + kv_width :]

    return (out_home, grad_in, grad_q, grad_k, grad_v, wo_sum)


def solution(mesh):
    in_specs = (
        P("dp", "fs"),
        P("dp", "fs"),
        P("dp", "fs"),
        P("dp", "fs"),
        P("dp", "fs"),
        P("fs", "dp"),
        P(),
        P("dp", None),
    )
    out_specs = (
        P("dp", "fs"),
        P("dp", "fs"),
        P("dp", "fs"),
        P("dp", "fs"),
        P("dp", "fs"),
        P("fs", "dp"),
    )
    return jax.shard_map(local, mesh=mesh, in_specs=in_specs, out_specs=out_specs, check_vma=False)
```

```python
import jax
import jax.numpy as jnp
from jax import lax
from jax.experimental import pallas as pl
from jax.experimental.pallas import tpu as pltpu
from jax.sharding import PartitionSpec as P

HS = 128
NZ, NX, NC = 4, 4, 2
theta_base = 1000000.0
f32 = jnp.float32
bf16 = jnp.bfloat16


def angles(position, width):
    freq = theta_base ** (-(jnp.arange(width // 2, dtype=jnp.float32) * 2.0) / width)
    phase = position.astype(jnp.float32)[:, None] * freq[None, :]
    return (jnp.cos(phase), jnp.sin(phase))


def rotated(values, cosine, sine):
    return values * cosine + pltpu.roll(values, HS // 2, 1) * sine


def unrotated(values, cosine, sine):
    return values * cosine - pltpu.roll(values, HS // 2, 1) * sine


def mask_of(first_length, count_rows):
    row = lax.broadcasted_iota(jnp.int32, (count_rows, count_rows), 0)
    col = lax.broadcasted_iota(jnp.int32, (count_rows, count_rows), 1)
    return (col <= row) & ((row >= first_length) == (col >= first_length))


def probs_of(query, keys, allowed):
    scores = nt(query, keys) * (HS ** (-0.5))
    scores = jnp.where(allowed, scores, -1e30)
    expo = jnp.exp(scores - jnp.max(scores, axis=-1, keepdims=True))
    return expo / jnp.sum(expo, axis=-1, keepdims=True)


def nt(left, right):
    return lax.dot_general(left, right, (((1,), (1,)), ((), ())), preferred_element_type=f32)


def tn(left, right):
    return lax.dot_general(left, right, (((0,), (0,)), ((), ())), preferred_element_type=f32)


def nn(left, right):
    return jnp.dot(left, right, preferred_element_type=f32)


def accumulate(step, pieces, w_refs, acc):
    own, above, far_one, far_two, below = pieces
    half = far_one.shape[0]
    low = 0
    for w_ref in w_refs:
        cols = slice(low, low + w_ref.shape[1])
        low += w_ref.shape[1]

        @pl.when(step == 0)
        def _():
            acc[:, cols] = nn(own[...], w_ref[...])

        @pl.when(step == 1)
        def _():
            acc[:, cols] += nn(above[...], w_ref[...])

        @pl.when(step == 2)
        def _():
            acc[:half, cols] += nn(far_one[...], w_ref[...])
            acc[half:, cols] += nn(far_two[...], w_ref[...])

        @pl.when(step == 3)
        def _():
            acc[:, cols] += nn(below[...], w_ref[...])


def forward_kernel(info, own, above, far_one, far_two, below, wq_ref, wkv_ref, cos_ref, sin_ref,
                   q_ref, k_ref, v_ref, flat_ref, acc):
    step = pl.program_id(0)
    accumulate(step, (own, above, far_one, far_two, below), (wq_ref, wkv_ref), acc)
    count_rows, q_width = q_ref.shape

    @pl.when(step == 3)
    def _():
        cosine, sine = cos_ref[...], sin_ref[...]
        keys = rotated(acc[:, q_width : q_width + HS], cosine, sine).astype(bf16)
        values = acc[:, q_width + HS :].astype(bf16)
        k_ref[...] = keys
        v_ref[...] = values
        allowed = mask_of(info[1], count_rows)
        for head in range(q_width // HS):
            cols = slice(head * HS, (head + 1) * HS)
            query = rotated(acc[:, cols], cosine, sine).astype(bf16)
            q_ref[:, cols] = query
            low = probs_of(query, keys, allowed).astype(bf16)
            flat_ref[:, cols] = nn(low, values).astype(bf16)


def backward_kernel(info, own, above, far_one, far_two, below, w_ref, cos_ref, sin_ref,
                    q_ref, k_ref, v_ref, flat_ref, grad_ref, acc):
    step = pl.program_id(0)
    accumulate(step, (own, above, far_one, far_two, below), (w_ref,), acc)
    count_rows, q_width = q_ref.shape

    @pl.when(step == 3)
    def _():
        cosine, sine = cos_ref[...], sin_ref[...]
        keys, values = k_ref[...], v_ref[...]
        allowed = mask_of(info[1], count_rows)
        d_keys = jnp.zeros((count_rows, HS), f32)
        d_values = jnp.zeros((count_rows, HS), f32)
        for head in range(q_width // HS):
            cols = slice(head * HS, (head + 1) * HS)
            query = q_ref[:, cols]
            d_att = acc[:, cols].astype(bf16)
            probs = probs_of(query, keys, allowed)
            delta = jnp.sum(
                d_att.astype(f32) * flat_ref[:, cols].astype(f32), axis=-1, keepdims=True
            )
            d_probs = nt(d_att, values)
            d_scores = (probs * (d_probs - delta) * (HS ** (-0.5))).astype(bf16)
            d_values += tn(probs.astype(bf16), d_att)
            d_keys += tn(d_scores, query)
            grad_ref[:, cols] = unrotated(nn(d_scores, keys), cosine, sine).astype(bf16)
        grad_ref[:, q_width : q_width + HS] = unrotated(d_keys, cosine, sine).astype(bf16)
        grad_ref[:, q_width + HS :] = d_values.astype(bf16)


def blocks_kernel(left_ref, w_ref, out_ref):
    out_ref[0] = nt(left_ref[...], w_ref[...]).astype(bf16)


def pair_kernel(left_ref, right_ref, came_a, came_b, *outs):
    lines, shard = came_a.shape[0] // 4, came_a.shape[0] // 16
    cut = came_a.shape[1]
    for at in range(4):
        rows = slice(at * lines, (at + 1) * lines)
        here = nn(left_ref[rows], right_ref[...])
        sum_a = (here[:, :cut] + came_a[rows].astype(f32)).astype(bf16)
        sum_b = (here[:, cut:] + came_b[rows].astype(f32)).astype(bf16)
        if at == 2:
            outs[2][...] = sum_a[: lines // 2].reshape(outs[2].shape)
            outs[3][...] = sum_a[lines // 2 :].reshape(outs[3].shape)
        else:
            place = {0: 0, 1: 1, 3: 4}[at]
            outs[place][...] = sum_a.reshape(outs[place].shape)
        for to in range(4):
            part = sum_b[to * shard : (to + 1) * shard]
            if to == 2:
                outs[7 if at < 2 else 8][at % 2] = part
            else:
                outs[{0: 5, 1: 6, 3: 9}[to]][at] = part


def join_kernel(one_a, three_a, down_a, up_a, one_b, three_b, down_b, up_b, *outs):
    for index, (one, three, down, up) in enumerate(
        ((one_a, three_a, down_a, up_a), (one_b, three_b, down_b, up_b))
    ):
        half = down.shape[0]
        to_one, to_three = outs[2 * index : 2 * index + 2]
        to_one[:half] = (one[:half].astype(f32) + down[...].astype(f32)).astype(bf16)
        to_one[half:] = one[half:]
        to_three[:half] = three[:half]
        to_three[half:] = (three[half:].astype(f32) + up[...].astype(f32)).astype(bf16)


def spread_kernel(info, left_ref, wq_ref, wkv_ref, own, one, far_one, far_two, three):
    step = pl.program_id(0)
    half = far_one.shape[0]
    q_width = wq_ref.shape[1]
    block = nt(left_ref[:, :q_width], wq_ref[...]) + nt(left_ref[:, q_width:], wkv_ref[...])
    block = block.astype(bf16)

    @pl.when(step == 0)
    def _():
        own[...] = block

    @pl.when(step == 1)
    def _():
        one[...] = block

    @pl.when(step == 2)
    def _():
        far_one[...] = block[:half]
        far_two[...] = block[half:]

    @pl.when(step == 3)
    def _():
        three[...] = block


def grad_out_kernel(info, own, above, far_one, far_two, below, flat_ref, out_ref):
    step = pl.program_id(0)
    half = far_one.shape[0]

    @pl.when(step == 0)
    def _():
        out_ref[...] = tn(own[...], flat_ref[...]).astype(bf16)

    @pl.when(step == 1)
    def _():
        out_ref[...] = tn(above[...], flat_ref[...]).astype(bf16)

    @pl.when(step == 2)
    def _():
        total = tn(far_one[...], flat_ref[:half]) + tn(far_two[...], flat_ref[half:])
        out_ref[...] = total.astype(bf16)

    @pl.when(step == 3)
    def _():
        out_ref[...] = tn(below[...], flat_ref[...]).astype(bf16)


def transpose_kernel(info, own, above, far_one, far_two, below, out_ref):
    step = pl.program_id(0)
    shard = out_ref.shape[3]

    def put(piece):
        turned = piece.T
        for at_x in range(4):
            for at_c in range(2):
                start = (at_x * 2 + at_c) * shard
                out_ref[(at_c + info[4]) % 2, 0, (at_x + 4 - info[3]) % 4] = (
                    turned[start : start + shard]
                )

    @pl.when(step == 0)
    def _():
        put(own[...])

    @pl.when(step == 1)
    def _():
        put(above[...])

    @pl.when(step == 2)
    def _():
        put(jnp.concatenate([far_one[...], far_two[...]], axis=0))

    @pl.when(step == 3)
    def _():
        put(below[...])


def fixed(array):
    zeros = (0,) * array.ndim
    return pl.BlockSpec(array.shape, lambda *_: zeros)


PARAMS = dict(compiler_params=pltpu.CompilerParams(vmem_limit_bytes=48 * 1024 * 1024))


def shape_of(*dims):
    return jax.ShapeDtypeStruct(dims, bf16)


def by_piece(kernel, info, operands, w, outs, out_specs, scratch):
    specs = [fixed(operand) for operand in operands]
    at = min(5, len(operands))

    def block_of(array, cols, place):
        return pl.BlockSpec((array.shape[0] // 4, cols), lambda k, s: ((s[0] + k) % 4, place))

    specs = specs[:at] + [block_of(*item) for item in w] + specs[at:]
    operands = operands[:at] + [item[0] for item in w] + operands[at:]
    return pl.pallas_call(
        kernel,
        out_shape=outs,
        grid_spec=pltpu.PrefetchScalarGridSpec(
            num_scalar_prefetch=1, grid=(4,), in_specs=specs, out_specs=out_specs,
            scratch_shapes=scratch,
        ),
        **PARAMS,
    )(info, *operands)


def by_block(left, w, cols, place):
    block = w.shape[0] // 4
    return pl.pallas_call(
        blocks_kernel,
        out_shape=shape_of(4, left.shape[0], block),
        grid=(4,),
        in_specs=[fixed(left), pl.BlockSpec((block, cols), lambda k: (k, place))],
        out_specs=pl.BlockSpec((1, left.shape[0], block), lambda k: (k, 0, 0)),
        **PARAMS,
    )(left, w)


def dp_index(z, x, c):
    return ((z % NZ) * NX + x % NX) * NC + c % NC


DP_ALL = [(z, x, c) for z in range(NZ) for x in range(NX) for c in range(NC)]
PERMS = {
    "z": lambda s: [(dp_index(z, x, c), dp_index(z + s, x, c)) for z, x, c in DP_ALL],
    "x": lambda s: [(dp_index(z, x, c), dp_index(z, x + s, c)) for z, x, c in DP_ALL],
    "core": lambda s: [(dp_index(z, x, c), dp_index(z, x, c + s)) for z, x, c in DP_ALL],
}


def shift(values, axis, step):
    if axis == "fs":
        return lax.ppermute(values, "fs", [(i, (i + step) % 4) for i in range(4)])
    return lax.ppermute(values, "dp", PERMS[axis](step))


def add(*terms):
    return sum([term.astype(f32) for term in terms]).astype(bf16)


def ring_first(own, axis):
    return shift(own, axis, 1), shift(own, axis, -1)


def ring_rest(own, first, axis):
    below, above = first
    half = own.shape[0] // 2
    return [own, above, shift(below[:half], axis, 1), shift(above[half:], axis, -1), below]


def together(*values):
    return lax.optimization_barrier(values)


def scatter_start(pieces, axis):
    return shift(pieces[2], axis, 1), shift(pieces[3], axis, -1)


def direct(pieces, axis):
    return [shift(pieces[r], axis, r) for r in (1, 2, 3)]


def after(values, first):
    return lax.optimization_barrier((values, first))[0]


def local(tokens, cotangent, w_query, w_key, w_value, w_out, route, doc_lengths):
    count_dp = lax.axis_size("dp")
    my_index = lax.axis_index("dp")
    my_fs = lax.axis_index("fs")
    my_z, my_x, my_c = my_index // 8, (my_index // 2) % 4, my_index % 2
    count_rows, width = tokens.shape
    piece_rows = count_rows // count_dp
    shard = w_query.shape[0]
    q_width, kv_width = w_query.shape[1], w_key.shape[1]

    w_all = lax.all_gather(
        jnp.concatenate([w_query, w_out.T, w_key, w_value], axis=1), "dp", axis=0, tiled=True
    )
    line_ids = jnp.arange(count_rows, dtype=jnp.int32)
    own_route = lax.dynamic_slice_in_dim(route, my_index * count_rows, count_rows)
    send_rank = jnp.sum((own_route[None, :] < own_route[:, None]).astype(jnp.int32), axis=1)
    send_table = (send_rank[None, :] == line_ids[:, None]).astype(bf16)

    planned = my_index * count_rows + line_ids
    home_block = jnp.arange(route.shape[0], dtype=jnp.int32) // count_rows
    source = jnp.sum(jnp.where(route[None, :] == planned[:, None], home_block[None, :], 0), axis=1)
    earlier = (source[None, :] == source[:, None]) & (line_ids[None, :] < line_ids[:, None])
    buffer_row = source * piece_rows + jnp.sum(earlier.astype(jnp.int32), axis=1)
    recv_table = (buffer_row[:, None] == line_ids[None, :]).astype(bf16)

    def outbound(values):
        moved = nn(send_table, values).astype(bf16)
        return moved.reshape(count_dp, piece_rows, values.shape[1])

    def inbound(values):
        return nn(recv_table, values.reshape(count_rows, values.shape[2])).astype(bf16)

    def swap(values):
        return lax.all_to_all(values, "dp", split_axis=0, concat_axis=0, tiled=True)

    def exchanged(blocks):
        return lax.all_to_all(blocks, "fs", split_axis=0, concat_axis=0, tiled=True)

    def total(came):
        return add(*[came[r] for r in range(4)])

    first_length = doc_lengths[0, 0]
    position = line_ids - jnp.where(line_ids >= first_length, first_length, 0)
    cosine, sine = angles(position, HS)
    cosine = jnp.concatenate([cosine, cosine], axis=1)
    sine = jnp.concatenate([-sine, sine], axis=1)
    info = jnp.stack([my_fs, first_length, my_z, my_x, my_c]).astype(jnp.int32)

    x_own = inbound(swap(outbound(tokens)))
    x_first = ring_first(x_own, "fs")
    c_own = inbound(swap(after(outbound(cotangent), x_own)))
    x_pieces = ring_rest(x_own, x_first, "fs")
    c_pieces = ring_rest(c_own, ring_first(c_own, "fs"), "fs")

    x_turned = by_piece(
        transpose_kernel, info, x_pieces, [],
        shape_of(2, 4, 4, shard, count_rows),
        pl.BlockSpec((2, 1, 4, shard, count_rows), lambda k, s: (0, (s[0] + k + 4 - s[2]) % 4, 0, 0, 0)),
        [],
    )
    own_t, other_t = [x_turned[i].reshape(16 * shard, count_rows) for i in range(2)]
    w_all, own_t, other_t, c_pieces = together(w_all, own_t, other_t, c_pieces)
    w_qkv = [(w_all, q_width, 0), (w_all, 2 * kv_width, q_width // kv_width)]
    w_out_t = [(w_all, q_width, 1)]

    rows_of = lambda cols: pl.BlockSpec((count_rows, cols), lambda *_: (0, 0))
    query, keys, values, flat = by_piece(
        forward_kernel, info, x_pieces + [cosine, sine], w_qkv,
        (shape_of(count_rows, q_width), shape_of(count_rows, kv_width),
         shape_of(count_rows, kv_width), shape_of(count_rows, q_width)),
        (rows_of(q_width), rows_of(kv_width), rows_of(kv_width), rows_of(q_width)),
        [pltpu.VMEM((count_rows, q_width + 2 * kv_width), f32)],
    )

    grad_out_part = by_piece(
        grad_out_kernel, info, c_pieces + [flat], [],
        shape_of(4 * width, q_width),
        pl.BlockSpec((width, q_width), lambda k, s: ((s[0] + k) % 4, 0)),
        [],
    )
    wo_sum = lax.psum_scatter(grad_out_part, "dp", scatter_dimension=0, tiled=True).T

    d_qkv = by_piece(
        backward_kernel, info,
        after(c_pieces, grad_out_part) + [cosine, sine, query, keys, values, flat], w_out_t,
        shape_of(count_rows, q_width + 2 * kv_width), rows_of(q_width + 2 * kv_width),
        [pltpu.VMEM((count_rows, q_width), f32)],
    )

    cut = 5 * HS
    cols = (d_qkv[:, :cut], d_qkv[:, cut:])
    there = [nn(other_t, part).astype(bf16) for part in cols]
    came = [shift(block, "core", 1) for block in there]
    head_blocks = by_block(after(flat, there), *w_out_t[0])
    out_came = exchanged(head_blocks)

    whole_array = lambda *arrays: [fixed(array) for array in arrays]
    shapes = []
    for part in cols:
        block = (4, shard, part.shape[1])
        shapes += [block, block, (2,) + block[1:], (2,) + block[1:], block]
    shapes = [shape_of(*dims) for dims in shapes]
    pair_in = (after(own_t, head_blocks), d_qkv, *came)
    pieces = pl.pallas_call(
        pair_kernel, out_shape=shapes, in_specs=whole_array(*pair_in),
        out_specs=whole_array(*shapes), grid=(1,), **PARAMS,
    )(*pair_in)
    pieces_a, pieces_b = pieces[:5], pieces[5:]
    step_a, step_b = scatter_start(pieces_a, "z"), scatter_start(pieces_b, "x")

    grad_blocks = by_piece(
        spread_kernel, info, [d_qkv], w_qkv,
        [shape_of(count_rows, width)] * 2 + [shape_of(count_rows // 2, width)] * 2
        + [shape_of(count_rows, width)],
        [rows_of(width)] * 2
        + [pl.BlockSpec((count_rows // 2, width), lambda *_: (0, 0))] * 2 + [rows_of(width)],
        [],
    )
    step_a, step_b, grad_blocks = together(step_a, step_b, grad_blocks)
    join_in = (pieces_a[1], pieces_a[4], *step_a, pieces_b[1], pieces_b[4], *step_b)
    join_out = [shapes[0]] * 2 + [shapes[5]] * 2
    one_a, three_a, one_b, three_b = pl.pallas_call(
        join_kernel, out_shape=join_out, in_specs=whole_array(*join_in),
        out_specs=whole_array(*join_out), grid=(1,), **PARAMS,
    )(*join_in)
    step_a = (shift(one_a, "z", 1), shift(three_a, "z", -1))
    step_b = (shift(one_b, "x", 1), shift(three_b, "x", -1))
    step_g = scatter_start(grad_blocks, "fs")
    going_home = tn(recv_table, total(after(out_came, one_a))).astype(bf16)
    returned = swap(going_home.reshape(count_dp, piece_rows, width))
    step_a, step_b, step_g = together(step_a, step_b, step_g)
    line_a, line_b = add(pieces_a[0], *step_a), add(pieces_b[0], *step_b)
    half = count_rows // 2
    one_g = jnp.concatenate([add(grad_blocks[1][:half], step_g[0]), grad_blocks[1][half:]], axis=0)
    three_g = jnp.concatenate(
        [grad_blocks[4][:half], add(grad_blocks[4][half:], step_g[1])], axis=0
    )
    step_g = (shift(one_g, "fs", 1), shift(three_g, "fs", -1))
    returned, step_g = together(after(returned, (line_a, line_b)), step_g)
    grad_in = add(grad_blocks[0], *step_g)
    out_home = tn(send_table, returned.reshape(count_rows, width)).astype(bf16)
    part_a = add(line_a[0], *direct(line_a, "x"))
    part_b = add(line_b[0], *direct(line_b, "z"))
    grad_q = jnp.concatenate([part_a, part_b[:, : q_width - cut]], axis=1)
    grad_k = part_b[:, q_width - cut : q_width - cut + kv_width]
    grad_v = part_b[:, q_width - cut + kv_width :]

    return (out_home, grad_in, grad_q, grad_k, grad_v, wo_sum)


def solution(mesh):
    in_specs = (
        P("dp", "fs"),
        P("dp", "fs"),
        P("dp", "fs"),
        P("dp", "fs"),
        P("dp", "fs"),
        P("fs", "dp"),
        P(),
        P("dp", None),
    )
    out_specs = (
        P("dp", "fs"),
        P("dp", "fs"),
        P("dp", "fs"),
        P("dp", "fs"),
        P("dp", "fs"),
        P("fs", "dp"),
    )
    return jax.shard_map(local, mesh=mesh, in_specs=in_specs, out_specs=out_specs, check_vma=False)
```
